256 devices in a mesh: fsdp: 16 (over x_lo, z), factor: 16 (over x_hi, y, core).
Axes of the slice: x: 4 (x_hi: 2, x_lo: 2; x = x_hi * 2 + x_lo), y: 4, z: 8, core: 2. Of those that a mesh axis runs over, the one named last changes fastest.
Arguments:
- activations: bfloat16 [256, 16, 16, 512], P(('fsdp', 'factor')), may hold values from -12 to 12
- cotangent: bfloat16 [256, 16, 16, 512], P(('fsdp', 'factor')), may hold values from -0.23632812 to 0.23632812
- weight: bfloat16 [4608, 512], P('fsdp'), may hold values from -0.09375 to 0.09375
- a_factor_old: float32 [4608, 4608], P('factor', 'fsdp'), may hold values from -0.11785113 to 5, as said below
- g_factor_old: float32 [512, 512], P('factor'), may hold values from -0.35355339 to 5, as said below
- a_inverse: float32 [4608, 4608], P('fsdp', 'factor'), may hold values from -0.09375 to 0.09375
- g_inverse: float32 [512, 512], replicated, may hold values from -0.25 to 0.25
Outputs:
- conv_out: bfloat16 [256, 16, 16, 512], P(('fsdp', 'factor'))
- a_factor: float32 [4608, 4608], P('factor', 'fsdp')
- g_factor: float32 [512, 512], P('factor')
- natural_grad: bfloat16 [4608, 512], P('fsdp', 'factor')
The draws below stay inside these ranges and needn't reach their ends.
Inputs may be any that keep to these rules, and one draw needn't show every extreme that they name: `a_factor_old`: a symmetric matrix. `g_factor_old`: a symmetric matrix.
All inputs are finite; a program needn't handle non-finite values.
Results may differ from the reference program's by a relative error of at most 0.0017.
Values may be sent and summed in bfloat16 or wider, within the bound.
A program may use at most 192 MiB of HBM per device.

```python
import math
import jax
import jax.numpy as jnp
from jax import lax

C = 512
FAN = 4608
S = 16
BATCH = 256
N_FACTOR = 16


def box_smooth(noise):
    side = noise.shape[1] - 2
    total = noise[:, 0:side, 0:side, :]
    for row_off in range(3):
        for col_off in range(3):
            if row_off + col_off > 0:
                total = total + noise[:, row_off:row_off + side, col_off:col_off + side, :]
    return total / 3.0


def textured_maps(key):
    keys = jax.random.split(key, 3)
    shape = (BATCH, S + 2, S + 2, C)
    noise = jax.random.normal(keys[0], shape, jnp.float32)
    field = box_smooth(noise)
    partner = jax.random.permutation(keys[1], C)
    mixed_field = (field + 0.6 * field[:, :, :, partner]) / math.sqrt(1.36)
    channel_scale = jnp.exp(jax.random.uniform(keys[2], (C,), jnp.float32, math.log(0.3), math.log(3.0)))
    result = mixed_field * channel_scale
    return jnp.clip(result, -12.0, 12.0)


def covariance_like(key, order):
    keys = jax.random.split(key, 2)
    diag_values = jnp.exp(jax.random.uniform(keys[0], (order,), jnp.float32, math.log(0.2), math.log(5.0)))
    raw = jax.random.normal(keys[1], (order, order), jnp.float32)
    spread = 1.2 / math.sqrt(order)
    symmetric = jnp.clip((raw + raw.T) * 0.70710678, -6.0, 6.0) * spread
    rows = jax.lax.broadcasted_iota(jnp.int32, (order, order), 0)
    cols = jax.lax.broadcasted_iota(jnp.int32, (order, order), 1)
    on_diag = rows == cols
    return jnp.where(on_diag, diag_values[:, None] * jnp.ones((1, order), jnp.float32), symmetric)


def draw_activations(key, part):
    return textured_maps(jax.random.fold_in(key, 11)).astype(jnp.bfloat16)


def draw_cotangent(key, part):
    maps = textured_maps(jax.random.fold_in(key, 23))
    image_ids = jax.lax.broadcasted_iota(jnp.int32, (BATCH, 1, 1, C), 0)
    channel_ids = jax.lax.broadcasted_iota(jnp.int32, (BATCH, 1, 1, C), 3)
    block_width = C // N_FACTOR
    owned = channel_ids // block_width == image_ids % N_FACTOR
    boost = jnp.where(owned, 5.0, 1.0).astype(jnp.float32)
    return (maps * boost / (S * math.sqrt(BATCH))).astype(jnp.bfloat16)


def draw_a_factor_old(key, part):
    return covariance_like(jax.random.fold_in(key, 37), 9 * C)


def draw_g_factor_old(key, part):
    return covariance_like(jax.random.fold_in(key, 41), C)


def levels(own_key, dims, cuts, smallest, largest):
    gain, own = 1.0, jax.random.fold_in(own_key, 6)
    for axis_at, blocks in cuts:
        steps = jnp.exp(jax.random.uniform(jax.random.fold_in(own, axis_at), (blocks,), jnp.float32, smallest / len(cuts), largest / len(cuts)))
        gain = gain * jnp.repeat(steps, dims[axis_at] // blocks).reshape([-1 if axis == axis_at else 1 for axis in range(len(dims))])
    return gain


def centred(own_key, shape, width, reach, shards=(), held_as=jnp.bfloat16):
    entries = width * jax.random.normal(own_key, shape, jnp.float32)
    if shards:
        entries = entries * levels(own_key, shape, shards, -0.22, 0.18)
    return jnp.clip(entries, -reach, reach).astype(held_as)


def setup_inputs(seed: int = 0) -> dict:
    splits = jax.random.split(jax.random.key(seed), 8)
    activations = draw_activations(jax.random.fold_in(splits[7], 71), 0)
    cotangent = draw_cotangent(jax.random.fold_in(splits[7], 71), 0)
    weight = centred(splits[2], (FAN, C), FAN ** -0.5, 0.09375, ((0, 16),))
    a_factor_old = draw_a_factor_old(jax.random.fold_in(splits[7], 71), 0)
    g_factor_old = draw_g_factor_old(jax.random.fold_in(splits[7], 71), 0)
    a_inverse = centred(splits[5], (FAN, FAN), FAN ** -0.5, 0.09375, ((0, 16), (1, 16)), jnp.float32)
    g_inverse = centred(splits[6], (C, C), C ** -0.5, 0.25, (), jnp.float32)
    return dict(activations=activations, cotangent=cotangent, weight=weight, a_factor_old=a_factor_old, g_factor_old=g_factor_old, a_inverse=a_inverse, g_inverse=g_inverse)


def unfold(images):
    padded = jnp.pad(images, ((0, 0), (1, 1), (1, 1), (0, 0)))
    tap_list = [padded[:, row_off:row_off + S, col_off:col_off + S, :] for row_off in range(3) for col_off in range(3)]
    return jnp.concatenate(tap_list, axis=3).reshape(-1, 9 * C)


def reference(activations, cotangent, weight, a_factor_old, g_factor_old, a_inverse, g_inverse):
    blocks = BATCH // 16
    act_blocks = activations.reshape(blocks, 16, S, S, C)
    cot_blocks = cotangent.reshape(blocks, 16, S, S, C)

    def block_step(carry, pieces):
        a_acc, grad_acc, g_acc = carry
        patches = unfold(pieces[0])
        cot_flat = pieces[1].reshape(-1, C)
        outputs = jnp.dot(patches, weight, preferred_element_type=jnp.float32).astype(jnp.bfloat16)
        a_acc = a_acc + jnp.dot(patches.T, patches, preferred_element_type=jnp.float32)
        grad_acc = grad_acc + jnp.dot(patches.T, cot_flat, preferred_element_type=jnp.float32)
        g_acc = g_acc + jnp.dot(cot_flat.T, cot_flat, preferred_element_type=jnp.float32)
        return (a_acc, grad_acc, g_acc), outputs.reshape(16, S, S, C)

    start_carry = (jnp.zeros((9 * C, 9 * C), jnp.float32), jnp.zeros((9 * C, C), jnp.float32), jnp.zeros((C, C), jnp.float32))
    (a_acc, grad_acc, g_acc), conv_blocks = lax.scan(block_step, start_carry, (act_blocks, cot_blocks))
    conv_out = conv_blocks.reshape(BATCH, S, S, C)
    pixel_total = float(BATCH * S * S)
    a_factor = 0.5 * a_factor_old + 0.5 * (a_acc / pixel_total)
    g_factor = 0.5 * g_factor_old + 0.5 * g_acc
    mixed = jnp.dot(grad_acc, g_inverse, precision=lax.Precision.HIGHEST, preferred_element_type=jnp.float32)
    natural_grad = jnp.dot(a_inverse, mixed, precision=lax.Precision.HIGHEST, preferred_element_type=jnp.float32).astype(jnp.bfloat16)
    return (conv_out, a_factor, g_factor, natural_grad)
```

```python
import jax
import jax.numpy as jnp
from jax import lax
from jax.experimental import pallas as pl
from jax.experimental.pallas import tpu as pltpu
from jax.sharding import PartitionSpec as P

MESH = pl.DeviceIdType.MESH
F32 = jnp.float32
BF16 = jnp.bfloat16
X_BLOCKS = ((0, 0), (1, 1), (2, 2), (0, 1), (0, 2), (1, 0), (2, 0))
Y_PAIRS = ((0, 0, 5), (1, 1, 5), (2, 2, 5), (0, 1, 7), (0, 2, 7))
BLOCKS = 29


def kernel(
    x_ref, dy_ref, w_ref, a_old_ref, g_old_ref, a_inv_ref, g_inv_ref,
    conv_ref, a_ref, g_ref, ng_ref,
    x_all, x_t, xa_t, xb, z_send, z_all, z_sh, w_all,
    m_part, m_recv, m_piece, m_rows, n_send, n_recv,
    a_send, a_recv, a_sum, tile, g_send, g_recv, g_sum, g2_recv, g_piece, g_fin,
    c_send, c_recv,
    in_sem, xs_sem, xr_sem, xf_sem, zs_sem, zr_sem, zf_sem, ws_sem, wr_sem,
    ms_sem, mr_sem, mgs_sem, mgr_sem, ns_sem, nr_sem, as_sem, ar_sem, ts_sem, tr_sem,
    gs_sem, gr_sem, g2s_sem, g2r_sem, g3s_sem, g3r_sem, cs_sem, cr_sem,
):
    i = lax.axis_index("fsdp")
    j = lax.axis_index("factor")
    xh, y, core = j // 8, (j // 2) % 4, j % 2
    a = 2 * xh + core
    b = y
    sibling = j + 1 - 2 * core

    def remote(src, dst, send, recv, dev_i, dev_j):
        return pltpu.make_async_remote_copy(
            src_ref=src, dst_ref=dst, send_sem=send, recv_sem=recv,
            device_id=(dev_i, dev_j), device_id_type=MESH,
        )

    def each(lo, hi, body):
        def step(k, carry):
            body(k)
            return carry
        lax.fori_loop(lo, hi, step, 0)

    entry = pltpu.get_barrier_semaphore()

    def greet(k):
        pl.semaphore_signal(entry, inc=1, device_id=((i + k) % 16, j), device_id_type=MESH)
        pl.semaphore_signal(entry, inc=1, device_id=(i, (j + k) % 16), device_id_type=MESH)

    each(1, 16, greet)
    pl.semaphore_wait(entry, 30)
    each(1, 16, lambda k: pl.semaphore_signal(
        in_sem, inc=1, device_id=(i, (j + k) % 16), device_id_type=MESH))

    def x_out(k):
        return remote(x_ref.at[0], x_all.at[pl.ds(1, 16), j], xs_sem.at[k], xr_sem.at[j],
                      i, (j + 2 * k) % 16)

    each(1, 8, lambda k: x_out(k).start())
    x_sib = remote(x_ref.at[0], x_all.at[pl.ds(1, 16), j], xs_sem.at[0], xr_sem.at[j], i, sibling)
    x_sib.start()

    def w_out(k):
        return remote(w_ref.at[:, pl.ds(pl.multiple_of(128 * y, 128), 128)],
                      w_all.at[pl.ds(pl.multiple_of(288 * i, 32), 288)],
                      ws_sem.at[k], wr_sem.at[i], (i + k) % 16, j)

    each(1, 16, lambda k: w_out(k).start())

    x_all[0] = jnp.zeros((16, 16, 512), BF16)
    x_all[17] = jnp.zeros((16, 16, 512), BF16)
    x_all[1:17, pl.ds(j, 1)] = x_ref[0][:, None]
    w_all[pl.ds(pl.multiple_of(288 * i, 32), 288), :] = w_ref[:, pl.ds(pl.multiple_of(128 * y, 128), 128)]

    cot = dy_ref[0].reshape(256, 512)
    g1 = g_inv_ref[...].astype(BF16)
    rest = g_inv_ref[...] - g1.astype(F32)
    g2 = rest.astype(BF16)
    g3 = (rest - g2.astype(F32)).astype(BF16)
    z = jnp.dot(cot, g3, preferred_element_type=F32)
    z = z + jnp.dot(cot, g2, preferred_element_type=F32)
    z = z + jnp.dot(cot, g1, preferred_element_type=F32)
    hi = z.astype(BF16)
    lo = (z - hi.astype(F32)).astype(BF16)
    for q in range(4):
        z_send[q, :, :, 0:128] = hi[:, 128 * q:128 * q + 128].reshape(16, 16, 128)
        z_send[q, :, :, 128:256] = lo[:, 128 * q:128 * q + 128].reshape(16, 16, 128)

    def z_out(k):
        to = (j + 2 * k) % 16
        return remote(z_send.at[(to // 2) % 4], z_all.at[:, j], zs_sem.at[k], zr_sem.at[j], i, to)

    each(1, 8, lambda k: z_out(k).start())
    z_sib = remote(z_send.at[y], z_all.at[:, j], zs_sem.at[0], zr_sem.at[j], i, sibling)
    z_sib.start()
    z_all[:, pl.ds(j, 1)] = z_send[y][:, None]

    g_send[...] = lax.dot_general(
        cot, cot, (((0,), (0,)), ((), ())), preferred_element_type=F32).astype(BF16)

    def g_out(k):
        to = (j + k) % 16
        return remote(g_send.at[pl.ds(pl.multiple_of(32 * to, 32), 32)], g_recv.at[j],
                      gs_sem.at[k], gr_sem.at[j], i, to)

    each(1, 16, lambda k: g_out(k).start())
    g_recv[pl.ds(j, 1)] = g_send[pl.ds(pl.multiple_of(32 * j, 32), 32)][None]

    def x_fwd(k):
        src = (j + 16 - 2 * k) % 16
        here = x_all.at[pl.ds(1, 16), src]
        return remote(here, here, xf_sem.at[k], xr_sem.at[src], i, sibling)

    def x_forward(k):
        x_fwd(k).wait_recv()
        x_fwd(k).start()

    def z_fwd(k):
        src = (j + 16 - 2 * k) % 16
        here = z_all.at[:, src]
        return remote(here, here, zf_sem.at[k], zr_sem.at[src], i, sibling)

    def z_forward(k):
        z_fwd(k).wait_recv()
        z_fwd(k).start()

    each(1, 8, x_forward)

    def x_other(k):
        src = (sibling + 2 * k) % 16
        here = x_all.at[pl.ds(1, 16), src]
        remote(here, here, xf_sem.at[0], xr_sem.at[src], i, sibling).wait_recv()

    each(0, 8, x_other)

    col = lax.broadcasted_iota(jnp.int32, (128, 256), 1) % 16
    row = lax.broadcasted_iota(jnp.int32, (256, 128), 0) % 16

    def plane(v):
        at = pl.ds(pl.multiple_of(256 * v, 256), 256)
        x_t[:, at] = x_all[v].reshape(256, 512).T
        mid = x_t[pl.ds(pl.multiple_of(128 * a, 128), 128), at]
        wide = mid.astype(F32)
        xa_t[0:128, at] = jnp.where(col == 0, 0.0, pltpu.roll(wide, 1, 1)).astype(BF16)
        xa_t[128:256, at] = mid
        xa_t[256:384, at] = jnp.where(col == 15, 0.0, pltpu.roll(wide, 255, 1)).astype(BF16)
        mid = x_all[v, :, :, pl.ds(pl.multiple_of(128 * b, 128), 128)].reshape(256, 128)
        wide = mid.astype(F32)
        xb[at, 0:128] = jnp.where(row == 0, 0.0, pltpu.roll(wide, 1, 0)).astype(BF16)
        xb[at, 128:256] = mid
        xb[at, 256:384] = jnp.where(row == 15, 0.0, pltpu.roll(wide, 255, 0)).astype(BF16)

    each(0, 18, plane)

    each(1, 8, z_forward)

    def z_other(k):
        src = (sibling + 2 * k) % 16
        here = z_all.at[:, src]
        remote(here, here, zf_sem.at[0], zr_sem.at[src], i, sibling).wait_recv()

    each(0, 8, z_other)

    row2 = lax.broadcasted_iota(jnp.int32, (256, 256), 0) % 16

    def z_plane(v):
        at = pl.ds(pl.multiple_of(256 * v, 256), 256)
        mid = z_all[v].reshape(256, 256)
        wide = mid.astype(F32)
        z_sh[0, at, :] = jnp.where(row2 == 15, 0.0, pltpu.roll(wide, 255, 0)).astype(BF16)
        z_sh[1, at, :] = mid
        z_sh[2, at, :] = jnp.where(row2 == 0, 0.0, pltpu.roll(wide, 1, 0)).astype(BF16)

    each(0, 16, z_plane)

    def m_chunk(k):
        r = 9 * a + k
        tap = r // 4
        lhs = x_t[pl.ds(pl.multiple_of(128 * (r % 4), 128), 128),
                  pl.ds(pl.multiple_of(256 * (tap // 3), 256), 4096)]
        both = jnp.dot(lhs, z_sh[tap % 3], preferred_element_type=F32)
        m_part[pl.ds(pl.multiple_of(128 * k, 128), 128), :] = both[:, 0:128] + both[:, 128:256]

    each(0, 9, m_chunk)

    def m_out(k):
        to = (i + k) % 16
        return remote(m_part.at[pl.ds(pl.multiple_of(72 * to, 8), 72)], m_recv.at[i],
                      ms_sem.at[k], mr_sem.at[i], to, j)

    each(1, 16, lambda k: m_out(k).start())
    m_recv[pl.ds(i, 1)] = m_part[pl.ds(pl.multiple_of(72 * i, 8), 72)][None]

    def a_out(to):
        return remote(a_send.at[pl.ds(pl.multiple_of(256 * to, 256), 256)], a_recv.at[i],
                      as_sem.at[to], ar_sem.at[i], to, j)

    def a_start(to):
        @pl.when(to != i)
        def _():
            a_out(to).start()

    at_block, sent = 0, 0
    for row_y, col_y, count in Y_PAIRS:
        part = jnp.dot(xa_t[:, 256 * row_y:256 * row_y + 4096],
                       xb[256 * col_y:256 * col_y + 4096, :], preferred_element_type=F32)
        for row_x, col_x in X_BLOCKS[:count]:
            a_send[128 * at_block:128 * at_block + 128, :] = part[
                128 * row_x:128 * row_x + 128, 128 * col_x:128 * col_x + 128].astype(BF16)
            at_block += 1
        if at_block == BLOCKS:
            a_send[128 * BLOCKS:128 * BLOCKS + 128, :] = jnp.zeros((128, 128), BF16)
            at_block += 1
        each(sent, at_block // 2, a_start)
        sent = at_block // 2

    @pl.when(i < 15)
    def _():
        a_recv[pl.ds(i, 1)] = a_send[pl.ds(pl.multiple_of(256 * i, 256), 256)][None]

    def w_in(k):
        src = (i + 16 - k) % 16
        here = w_all.at[pl.ds(pl.multiple_of(288 * src, 32), 288)]
        remote(here, here, ws_sem.at[k], wr_sem.at[src], src, j).wait_recv()

    each(1, 16, w_in)
    conv_row = lax.broadcasted_iota(jnp.int32, (256, 128), 0) % 16

    def conv_image(q):
        image = 8 * xh + 2 * q + core
        parts = []
        for dx in range(3):
            total = jnp.zeros((256, 128), F32)
            for dy in range(3):
                total = total + jnp.dot(
                    x_all[dy:dy + 16, pl.ds(image, 1)].reshape(256, 512),
                    w_all[512 * (3 * dy + dx):512 * (3 * dy + dx) + 512, :],
                    preferred_element_type=F32)
            parts.append(total)
        out = parts[1] + jnp.where(conv_row == 0, 0.0, pltpu.roll(parts[0], 1, 0))
        out = out + jnp.where(conv_row == 15, 0.0, pltpu.roll(parts[2], 255, 0))
        c_send[pl.ds(q, 1)] = out.astype(BF16)[None]

    each(0, 4, conv_image)
    here_y = pl.ds(pl.multiple_of(128 * y, 128), 128)

    def c_out(k):
        q = (y + k) % 4
        return remote(c_send.at[q], c_recv.at[:, here_y], cs_sem.at[k], cr_sem.at[y],
                      i, 8 * xh + 2 * q + core)

    each(1, 4, lambda k: c_out(k).start())
    c_recv[:, here_y] = c_send[y]

    def m_in(k):
        src = (i + 16 - k) % 16
        here = m_recv.at[src]
        remote(here, here, ms_sem.at[k], mr_sem.at[src], src, j).wait_recv()

    each(1, 16, m_in)
    total = m_recv[0]
    for k in range(1, 16):
        total = total + m_recv[k]
    m_piece[...] = total
    pl.semaphore_wait(in_sem, 15)
    m_to = 4 * a + i // 4

    def m_spot(rho, chunk):
        return m_rows.at[pl.ds(pl.multiple_of(72 * rho, 8), 72),
                         pl.ds(pl.multiple_of(128 * chunk, 128), 128)]

    def mg_out(to):
        return remote(m_piece, m_spot(i % 4, b), mgs_sem.at[to], mgr_sem.at[4 * (i % 4) + b], to, m_to)

    def mg_self():
        return pltpu.make_async_copy(m_piece, m_spot(i % 4, b), mgr_sem.at[4 * (i % 4) + b])

    def mg_start(k):
        to = (i + k) % 16
        mine = (to == i) & (m_to == j)

        @pl.when(jnp.logical_not(mine))
        def _():
            mg_out(to).start()

        @pl.when(mine)
        def _():
            mg_self().start()

    each(0, 16, mg_start)

    def g_in(k):
        src = (j + 16 - k) % 16
        here = g_recv.at[src]
        remote(here, here, gs_sem.at[k], gr_sem.at[src], i, src).wait_recv()

    each(1, 16, g_in)
    total = g_recv[0].astype(F32)
    for k in range(1, 16):
        total = total + g_recv[k].astype(F32)
    g_sum[...] = total

    def g_spot(ref, who):
        return ref.at[pl.ds(pl.multiple_of(8 * (who // 4), 8), 8),
                      pl.ds(pl.multiple_of(128 * (who % 4), 128), 128)]

    def g2_out(k):
        to = (i + k) % 16
        return remote(g_spot(g_sum, to), g2_recv.at[i], g2s_sem.at[k], g2r_sem.at[i], to, j)

    each(1, 16, lambda k: g2_out(k).start())
    g2_recv[pl.ds(i, 1)] = g_sum[pl.ds(pl.multiple_of(8 * (i // 4), 8), 8),
                                 pl.ds(pl.multiple_of(128 * (i % 4), 128), 128)][None]

    @pl.when(i < 15)
    def _():
        def a_in(k):
            src = (i + 16 - k) % 16
            here = a_recv.at[src]
            remote(here, here, as_sem.at[0], ar_sem.at[src], src, j).wait_recv()

        each(1, 16, a_in)
        for half in range(2):
            span = slice(128 * half, 128 * half + 128)
            total = a_recv[0, span].astype(F32)
            for k in range(1, 16):
                total = total + a_recv[k, span].astype(F32)
            a_sum[2 * half] = total
            a_sum[2 * half + 1] = total.T

    def spread(act):
        def one(n):
            half = n // 32
            turned = (n // 16) % 2
            yp, xp, tj, ti = (n // 8) % 2, (n // 4) % 2, (n // 2) % 2, n % 2
            k = 2 * i + half
            flat = k < 15
            ey = jnp.where(flat, 0, jnp.where(k < 22, 1, 2))
            s = jnp.where(flat, k % 5, (k + 6) % 7)
            ex = jnp.where(s < 3, 0, jnp.where(s < 5, s - 2, 4 - s))
            row_y = jnp.where(flat, k // 5, yp)
            row_x = jnp.where(s < 3, s, jnp.where(s < 5, 0, s - 4)) + xp
            ok = (k < BLOCKS) & ((yp == 0) | (ey == 1)) & ((xp == 0) | (ex == 1) | (ex == -1))
            ok = ok & ((turned == 0) | (ey != 0) | (ex != 0))
            first = 4 * (3 * row_y + row_x) + a
            second = 4 * (3 * (row_y + ey) + row_x + ex) + b
            r = jnp.where(turned == 0, first, second)
            c = jnp.where(turned == 0, second, first)
            to_j = (4 * r) // 9 + tj
            to_i = (4 * c) // 9 + ti
            ok = ok & (to_j <= (128 * r + 127) // 288) & (to_i <= (128 * c + 127) // 288)
            at_r = r - (9 * to_j) // 4
            at_c = c - (9 * to_i) // 4
            src = a_sum.at[2 * half + turned]
            dst = tile.at[pl.ds(pl.multiple_of(128 * at_r, 128), 128),
                          pl.ds(pl.multiple_of(128 * at_c, 128), 128)]
            mine = (to_i == i) & (to_j == j)
            arrived = tr_sem.at[3 * at_r + at_c]

            @pl.when(ok & jnp.logical_not(mine))
            def _():
                act(remote(src, dst, ts_sem.at[n], arrived, to_i, to_j))

            if act is start:
                @pl.when(ok & mine)
                def _():
                    pltpu.make_async_copy(src, dst, arrived).start()

        each(0, 64, one)

    def start(copy):
        copy.start()

    def sent_off(copy):
        copy.wait_send()

    spread(start)

    for q in range(4):
        for chunk in range(4):
            here = m_spot(q, chunk)
            remote(here, here, mgs_sem.at[0], mgr_sem.at[4 * q + chunk], i, sibling).wait_recv()
    prod = jnp.dot(a_inv_ref[...], m_rows[...], precision=lax.Precision.HIGHEST,
                   preferred_element_type=F32)
    lane = lax.broadcasted_iota(jnp.int32, (72, 128), 1) // 32
    for to in range(16):
        piece = jnp.zeros((72, 128), F32)
        for q in range(4):
            block = prod[72 * q:72 * q + 72, 128 * (to // 4):128 * (to // 4) + 128]
            shift = (32 * (q - to % 4)) % 128
            if shift:
                block = pltpu.roll(block, shift, 1)
            piece = jnp.where(lane == q, block, piece)
        n_send[to] = piece

    def n_out(k):
        to = (j + k) % 16
        return remote(n_send.at[to], n_recv.at[j], ns_sem.at[k], nr_sem.at[j], i, to)

    each(1, 16, lambda k: n_out(k).start())
    n_recv[pl.ds(j, 1)] = n_send[pl.ds(j, 1)]

    def g2_in(k):
        src = (i + 16 - k) % 16
        here = g2_recv.at[src]
        remote(here, here, g2s_sem.at[k], g2r_sem.at[src], src, j).wait_recv()

    each(1, 16, g2_in)
    total = g2_recv[0]
    for k in range(1, 16):
        total = total + g2_recv[k]
    g_piece[...] = total

    def g3_out(k):
        return remote(g_piece, g_spot(g_fin, i), g3s_sem.at[k], g3r_sem.at[i], (i + k) % 16, j)

    each(1, 16, lambda k: g3_out(k).start())
    g_fin[pl.ds(pl.multiple_of(8 * (i // 4), 8), 8),
          pl.ds(pl.multiple_of(128 * (i % 4), 128), 128)] = total

    def c_in(k):
        q = (y + 4 - k) % 4
        here = c_recv.at[:, pl.ds(pl.multiple_of(128 * q, 128), 128)]
        remote(here, here, cs_sem.at[k], cr_sem.at[q], i, sibling).wait_recv()

    each(1, 4, c_in)
    conv_ref[...] = c_recv[...]

    for q in range(9):
        here = tile.at[pl.ds(128 * (q // 3), 128), pl.ds(128 * (q % 3), 128)]
        remote(here, here, ts_sem.at[0], tr_sem.at[q], i, sibling).wait_recv()
    rows = tile[pl.ds(pl.multiple_of(32 * (j % 4), 32), 288), :]
    rows = pltpu.roll(rows, (384 - 32 * (i % 4)) % 384, 1)[:, 0:288]
    a_ref[...] = 0.5 * a_old_ref[...] + (0.5 / 65536.0) * rows

    def g3_in(k):
        src = (i + 16 - k) % 16
        here = g_spot(g_fin, src)
        remote(here, here, g3s_sem.at[k], g3r_sem.at[src], src, j).wait_recv()

    each(1, 16, g3_in)
    g_ref[...] = 0.5 * g_old_ref[...] + 0.5 * g_fin[...]

    def n_in(k):
        src = (j + 16 - k) % 16
        here = n_recv.at[src]
        remote(here, here, ns_sem.at[k], nr_sem.at[src], i, src).wait_recv()

    each(1, 16, n_in)
    total = n_recv[0]
    for k in range(1, 16):
        total = total + n_recv[k]
    ng_ref[...] = total

    x_sib.wait_send()
    z_sib.wait_send()
    each(1, 8, lambda k: x_out(k).wait_send())
    each(1, 8, lambda k: z_out(k).wait_send())
    each(1, 8, lambda k: x_fwd(k).wait_send())
    each(1, 8, lambda k: z_fwd(k).wait_send())
    each(1, 4, lambda k: c_out(k).wait_send())

    def rest_sent(k):
        w_out(k).wait_send()
        g_out(k).wait_send()
        m_out(k).wait_send()
        g2_out(k).wait_send()
        g3_out(k).wait_send()
        n_out(k).wait_send()

    each(1, 16, rest_sent)

    def a_sent(to):
        @pl.when(to != i)
        def _():
            a_out(to).wait_send()

    each(0, 15, a_sent)

    def mg_sent(to):
        @pl.when(jnp.logical_not((to == i) & (m_to == j)))
        def _():
            mg_out(to).wait_send()

    each(0, 16, mg_sent)
    spread(sent_off)


def per_device(activations, cotangent, weight, a_factor_old, g_factor_old, a_inverse, g_inverse):
    vmem = pl.BlockSpec(memory_space=pltpu.VMEM)
    dma = pltpu.SemaphoreType.DMA
    conv, a_factor, g_factor, packed = pl.pallas_call(
        kernel,
        name="kfac_step",
        out_shape=(
            jax.ShapeDtypeStruct((256, 512), BF16),
            jax.ShapeDtypeStruct((288, 288), F32),
            jax.ShapeDtypeStruct((32, 512), F32),
            jax.ShapeDtypeStruct((72, 128), F32),
        ),
        in_specs=[vmem] * 7,
        out_specs=(vmem,) * 4,
        scratch_shapes=[
            pltpu.VMEM((18, 16, 16, 512), BF16),
            pltpu.VMEM((512, 4608), BF16),
            pltpu.VMEM((384, 4608), BF16),
            pltpu.VMEM((4608, 384), BF16),
            pltpu.VMEM((4, 16, 16, 256), BF16),
            pltpu.VMEM((16, 16, 16, 256), BF16),
            pltpu.VMEM((3, 4096, 256), BF16),
            pltpu.VMEM((4608, 128), BF16),
            pltpu.VMEM((1152, 128), F32),
            pltpu.VMEM((16, 72, 128), F32),
            pltpu.VMEM((72, 128), F32),
            pltpu.VMEM((288, 512), F32),
            pltpu.VMEM((16, 72, 128), F32),
            pltpu.VMEM((16, 72, 128), F32),
            pltpu.VMEM((3840, 128), BF16),
            pltpu.VMEM((16, 256, 128), BF16),
            pltpu.VMEM((4, 128, 128), F32),
            pltpu.VMEM((384, 384), F32),
            pltpu.VMEM((512, 512), BF16),
            pltpu.VMEM((16, 32, 512), BF16),
            pltpu.VMEM((32, 512), F32),
            pltpu.VMEM((16, 8, 128), F32),
            pltpu.VMEM((8, 128), F32),
            pltpu.VMEM((32, 512), F32),
            pltpu.VMEM((4, 256, 128), BF16),
            pltpu.VMEM((256, 512), BF16),
            pltpu.SemaphoreType.REGULAR,
            dma((8,)), dma((16,)), dma((8,)),
            dma((8,)), dma((16,)), dma((8,)),
            dma((16,)), dma((16,)),
            dma((16,)), dma((16,)), dma((16,)), dma((16,)),
            dma((16,)), dma((16,)),
            dma((16,)), dma((16,)), dma((64,)), dma((9,)),
            dma((16,)), dma((16,)), dma((16,)), dma((16,)), dma((16,)), dma((16,)),
            dma((4,)), dma((4,)),
        ],
        compiler_params=pltpu.CompilerParams(
            collective_id=0, has_side_effects=True, vmem_limit_bytes=56 * 1024 * 1024),
        cost_estimate=pl.CostEstimate(flops=15_000_000_000, bytes_accessed=4_000_000, transcendentals=0),
    )(activations, cotangent, weight, a_factor_old, g_factor_old, a_inverse, g_inverse)
    natural = packed.reshape(72, 4, 32).transpose(1, 0, 2).reshape(288, 32).astype(BF16)
    return conv.reshape(1, 16, 16, 512), a_factor, g_factor, natural


def solution(mesh):
    return jax.shard_map(
        per_device,
        mesh=mesh,
        in_specs=(
            P(("fsdp", "factor"), None, None, None),
            P(("fsdp", "factor"), None, None, None),
            P("fsdp", None),
            P("factor", "fsdp"),
            P("factor", None),
            P("fsdp", "factor"),
            P(),
        ),
        out_specs=(
            P(("fsdp", "factor"), None, None, None),
            P("factor", "fsdp"),
            P("factor", None),
            P("fsdp", "factor"),
        ),
        check_vma=False,
    )
```

```python
import jax
import jax.numpy as jnp
from jax import lax
from jax.experimental import pallas as pl
from jax.experimental.pallas import tpu as pltpu
from jax.sharding import PartitionSpec as P

MESH = pl.DeviceIdType.MESH
F32 = jnp.float32
BF16 = jnp.bfloat16
X_BLOCKS = ((0, 0), (1, 1), (2, 2), (0, 1), (0, 2), (1, 0), (2, 0))
COUNTS = (5, 5, 5, 7, 7)
BLOCKS = 29


def kernel(
    x_ref, dy_ref, w_ref, a_old_ref, g_old_ref, a_inv_ref, g_inv_ref,
    conv_ref, a_ref, g_ref, ng_ref,
    x_all, x_t, xa_t, xb, z_all, z_sh, w_all, a_acc, inv_both,
    m_part, m_recv, m_cols, m_piece, m_rows, n_send, n_recv,
    a_send, a_recv, a_sum, tile, g_send, g_recv, g_sum, g2_recv, g_piece, g_fin,
    c_send, c_recv,
    in_sem, inv_sem, xs_sem, xr_sem, xh_sem, xf_sem, zs_sem, zr_sem, zf_sem, ws_sem, wr_sem, wf_sem,
    ms_sem, mr_sem, mxs_sem, mxr_sem, mgs_sem, mgr_sem, ns_sem, nr_sem, as_sem, ar_sem, ts_sem, tr_sem,
    gs_sem, gr_sem, g2s_sem, g2r_sem, g3s_sem, g3r_sem, cs_sem, cr_sem,
):
    i = lax.axis_index("fsdp")
    j = lax.axis_index("factor")
    xh, y, core = j // 8, (j // 2) % 4, j % 2
    a = 2 * xh + core
    b = y
    sibling = j + 1 - 2 * core
    xl, z = i // 8, i % 8

    def remote(src, dst, send, recv, dev_i, dev_j):
        return pltpu.make_async_remote_copy(
            src_ref=src, dst_ref=dst, send_sem=send, recv_sem=recv,
            device_id=(dev_i, dev_j), device_id_type=MESH,
        )

    def each(lo, hi, body):
        def step(k, carry):
            body(k)
            return carry
        lax.fori_loop(lo, hi, step, 0)

    entry = pltpu.get_barrier_semaphore()

    def greet(k):
        pl.semaphore_signal(entry, inc=1, device_id=((i + k) % 16, j), device_id_type=MESH)
        pl.semaphore_signal(entry, inc=1, device_id=(i, (j + k) % 16), device_id_type=MESH)

    each(1, 16, greet)
    pl.semaphore_wait(entry, 30)
    each(1, 16, lambda k: pl.semaphore_signal(
        in_sem, inc=1, device_id=(i, (j + k) % 16), device_id_type=MESH))

    def image(half, step):
        return 8 * ((xh + half) % 2) + 2 * ((y + step + 4) % 4) + core

    def x_at(who, lo=0, size=256):
        return x_all.at[who, pl.ds(16 + lo, size)]

    def x_own(n):
        to = (image(0, 1), image(0, -1), image(1, 0), sibling)[n]
        return remote(x_ref, x_at(j), xs_sem.at[n], xr_sem.at[j], i, to)

    def x_pass(n):
        who = image(1, 0)
        return remote(x_at(who), x_at(who), xs_sem.at[4 + n], xr_sem.at[who], i, image(0, 1 - 2 * n))

    def x_half(half, n):
        step = 1 - 2 * n
        who = image(half, -step)
        here = x_at(who, 128 * n, 128)
        return remote(here, here, xs_sem.at[6 + 2 * half + n], (xr_sem, xh_sem)[n].at[who], i, image(0, step))

    def x_fwd(who):
        return remote(x_at(who), x_at(who), xf_sem.at[who], xr_sem.at[who], i, sibling)

    def x_got(who, lo=0, size=256, sem=None):
        here = x_at(who, lo, size)
        remote(here, here, xf_sem.at[who], (xr_sem if sem is None else sem).at[who], i, sibling).wait_recv()

    for n in range(4):
        x_own(n).start()

    def z_out(k):
        to = (j + 2 * k) % 16
        return remote(dy_ref.at[:, pl.ds(pl.multiple_of(128 * ((to // 2) % 4), 128), 128)],
                      z_all.at[j], zs_sem.at[k], zr_sem.at[j], i, to)

    each(1, 8, lambda k: z_out(k).start())
    here_y = pl.ds(pl.multiple_of(128 * y, 128), 128)
    z_sib = remote(dy_ref.at[:, here_y], z_all.at[j], zs_sem.at[0], zr_sem.at[j], i, sibling)
    z_sib.start()

    def w_at(who):
        return w_all.at[pl.ds(pl.multiple_of(288 * who, 32), 288)]

    def w_out(k):
        return remote(w_ref.at[:, here_y], w_at(i), ws_sem.at[k], wr_sem.at[i], (i + k) % 16, j)

    w_lo = 2 - core

    def w_each(body):
        def step(n, carry):
            body(2 * n + w_lo)
            return carry
        lax.fori_loop(0, 7 + core, step, 0)

    w_each(lambda k: w_out(k).start())

    inv_out = remote(a_inv_ref, inv_both.at[xl], inv_sem.at[0], inv_sem.at[1], (i + 8) % 16, j)
    inv_out.start()

    def clear(who):
        x_all[pl.ds(who, 1), 0:16] = jnp.zeros((1, 16, 512), BF16)
        x_all[pl.ds(who, 1), 272:288] = jnp.zeros((1, 16, 512), BF16)

    each(0, 16, clear)
    x_all[pl.ds(j, 1), 16:272] = x_ref[...][None]
    z_all[pl.ds(j, 1)] = dy_ref[:, here_y][None]
    w_all[pl.ds(pl.multiple_of(288 * i, 32), 288), :] = w_ref[:, here_y]
    inv_both[pl.ds(xl, 1)] = a_inv_ref[...][None]
    xb[256:288, :] = jnp.zeros((32, 384), BF16)
    for dx in range(3):
        z_sh[dx, 0:16] = jnp.zeros((16, 128), BF16)
        z_sh[dx, 272:288] = jnp.zeros((16, 128), BF16)
    a_acc[...] = jnp.zeros((5, 384, 384), F32)
    m_part[...] = jnp.zeros((1152, 128), F32)

    col = lax.broadcasted_iota(jnp.int32, (128, 256), 1) % 16
    row = lax.broadcasted_iota(jnp.int32, (256, 128), 0) % 16
    map_row = lax.broadcasted_iota(jnp.int32, (256, 384), 0) // 16
    none = jnp.zeros((256, 384), BF16)

    def terms(who):
        x_t[...] = x_all[pl.ds(who, 1), 16:272].reshape(256, 512).T
        mid = x_t[pl.ds(pl.multiple_of(128 * a, 128), 128), :]
        wide = mid.astype(F32)
        xa_t[0:128] = jnp.where(col == 0, 0.0, pltpu.roll(wide, 1, 1)).astype(BF16)
        xa_t[128:256] = mid
        xa_t[256:384] = jnp.where(col == 15, 0.0, pltpu.roll(wide, 255, 1)).astype(BF16)
        mid = x_all[pl.ds(who, 1), 16:272, here_y].reshape(256, 128)
        wide = mid.astype(F32)
        xb[0:256, 0:128] = jnp.where(row == 0, 0.0, pltpu.roll(wide, 1, 0)).astype(BF16)
        xb[0:256, 128:256] = mid
        xb[0:256, 256:384] = jnp.where(row == 15, 0.0, pltpu.roll(wide, 255, 0)).astype(BF16)
        mid = z_all[pl.ds(who, 1)].reshape(256, 128)
        wide = mid.astype(F32)
        z_sh[0, 16:272] = jnp.where(row == 15, 0.0, pltpu.roll(wide, 255, 0)).astype(BF16)
        z_sh[1, 16:272] = mid
        z_sh[2, 16:272] = jnp.where(row == 0, 0.0, pltpu.roll(wide, 1, 0)).astype(BF16)
        lhs = xa_t[...]
        flat = xb[0:256, :]
        a_acc[0] += jnp.dot(lhs, jnp.where(map_row == 15, none, flat), preferred_element_type=F32)
        a_acc[1] += jnp.dot(lhs, flat, preferred_element_type=F32)
        a_acc[2] += jnp.dot(lhs, jnp.where(map_row == 0, none, flat), preferred_element_type=F32)
        a_acc[3] += jnp.dot(lhs, xb[16:272, :], preferred_element_type=F32)
        a_acc[4] += jnp.dot(lhs, xb[32:288, :], preferred_element_type=F32)
        for k in range(9):
            r = 9 * a + k
            tap = r // 4
            part = jnp.dot(x_t[pl.ds(pl.multiple_of(128 * (r % 4), 128), 128), :],
                           z_sh[tap % 3, pl.ds(pl.multiple_of(32 - 16 * (tap // 3), 16), 256), :],
                           preferred_element_type=F32)
            m_part[128 * k:128 * k + 128, :] += part

    def z_fwd(who):
        return remote(z_all.at[who], z_all.at[who], zf_sem.at[who // 2], zr_sem.at[who], i, sibling)

    def z_got(who):
        remote(z_all.at[who], z_all.at[who], zf_sem.at[0], zr_sem.at[who], i, sibling).wait_recv()

    def hand_on(who):
        x_fwd(who).start()
        z_got(who)
        z_fwd(who).start()

    def from_ring(half, n):
        x_got(image(half, 2 * n - 1))
        x_half(half, n).start()
        hand_on(image(half, 2 * n - 1))

    def from_far(half):
        who = image(half, 2)
        x_got(who, 0, 128)
        x_got(who, 128, 128, xh_sem)
        hand_on(who)

    def arrivals(n, carry):
        @pl.when(n == 1)
        def _():
            from_ring(0, 0)
            from_ring(0, 1)
            x_got(image(1, 0))
            x_pass(0).start()
            x_pass(1).start()
            hand_on(image(1, 0))

        @pl.when(n == 3)
        def _():
            from_far(0)

        @pl.when(n == 5)
        def _():
            from_ring(1, 0)
            from_ring(1, 1)

        @pl.when(n == 7)
        def _():
            from_far(1)

        half = jnp.where((n == 3) | (n > 4), 1, 0)
        step = jnp.where((n == 0) | (n == 3), 0, jnp.where((n == 1) | (n == 5), 3, jnp.where((n == 2) | (n == 6), 1, 2)))
        mine = image(half, step)

        def one(c, carry):
            who = jnp.where(c == 0, mine, mine + 1 - 2 * core)

            @pl.when(c == 1)
            def _():
                x_got(who)
                z_got(who)

            terms(who)
            return carry

        return lax.fori_loop(0, 2, one, carry)

    lax.fori_loop(0, 8, arrivals, 0)

    def w_in(k):
        src = (i + 16 - k) % 16
        remote(w_at(src), w_at(src), ws_sem.at[k], wr_sem.at[src], src, j).wait_recv()

    def w_fwd(k):
        src = (i + 16 - k) % 16
        return remote(w_at(src), w_at(src), wf_sem.at[k], wr_sem.at[src], i, sibling)

    def w_forward(k):
        w_in(k)
        w_fwd(k).start()

    w_each(w_forward)

    def m_out(k):
        to = (i + k) % 16
        return remote(m_part.at[pl.ds(pl.multiple_of(72 * to, 8), 72)], m_recv.at[i],
                      ms_sem.at[k], mr_sem.at[i], to, j)

    each(1, 16, lambda k: m_out(k).start())
    m_recv[pl.ds(i, 1)] = m_part[pl.ds(pl.multiple_of(72 * i, 8), 72)][None]

    cot = dy_ref[...]
    g_send[...] = lax.dot_general(
        cot, cot, (((0,), (0,)), ((), ())), preferred_element_type=F32).astype(BF16)

    def g_out(k):
        to = (j + k) % 16
        return remote(g_send.at[pl.ds(pl.multiple_of(32 * to, 32), 32)], g_recv.at[j],
                      gs_sem.at[k], gr_sem.at[j], i, to)

    each(1, 16, lambda k: g_out(k).start())
    g_recv[pl.ds(j, 1)] = g_send[pl.ds(pl.multiple_of(32 * j, 32), 32)][None]

    def a_out(to):
        return remote(a_send.at[pl.ds(pl.multiple_of(256 * to, 256), 256)], a_recv.at[i],
                      as_sem.at[to], ar_sem.at[i], to, j)

    def a_start(to):
        @pl.when(to != i)
        def _():
            a_out(to).start()

    at_block, sent = 0, 0
    for combo, count in enumerate(COUNTS):
        part = a_acc[combo]
        for row_x, col_x in X_BLOCKS[:count]:
            a_send[128 * at_block:128 * at_block + 128, :] = part[
                128 * row_x:128 * row_x + 128, 128 * col_x:128 * col_x + 128].astype(BF16)
            at_block += 1
        if at_block == BLOCKS:
            a_send[128 * BLOCKS:128 * BLOCKS + 128, :] = jnp.zeros((128, 128), BF16)
            at_block += 1
        each(sent, at_block // 2, a_start)
        sent = at_block // 2

    @pl.when(i < 15)
    def _():
        a_recv[pl.ds(i, 1)] = a_send[pl.ds(pl.multiple_of(256 * i, 256), 256)][None]

    def w_other(k):
        @pl.when(k % 2 != core)
        def _():
            w_in(k)

    each(1, 16, w_other)
    conv_row = lax.broadcasted_iota(jnp.int32, (256, 128), 0) % 16

    def conv_image(q):
        who = 8 * xh + 2 * q + core
        parts = []
        for dx in range(3):
            total = jnp.zeros((256, 128), F32)
            for dy in range(3):
                total = total + jnp.dot(
                    x_all[pl.ds(who, 1), 16 * dy:16 * dy + 256].reshape(256, 512),
                    w_all[512 * (3 * dy + dx):512 * (3 * dy + dx) + 512, :],
                    preferred_element_type=F32)
            parts.append(total)
        out = parts[1] + jnp.where(conv_row == 0, 0.0, pltpu.roll(parts[0], 1, 0))
        out = out + jnp.where(conv_row == 15, 0.0, pltpu.roll(parts[2], 255, 0))
        c_send[pl.ds(q, 1)] = out.astype(BF16)[None]

    each(0, 4, conv_image)

    def c_out(k):
        q = (y + k) % 4
        return remote(c_send.at[q], c_recv.at[:, here_y], cs_sem.at[k], cr_sem.at[y],
                      i, 8 * xh + 2 * q + core)

    each(1, 4, lambda k: c_out(k).start())
    c_recv[:, here_y] = c_send[y]

    def m_in(k):
        src = (i + 16 - k) % 16
        here = m_recv.at[src]
        remote(here, here, ms_sem.at[k], mr_sem.at[src], src, j).wait_recv()

    each(1, 16, m_in)
    total = m_recv[0]
    for k in range(1, 16):
        total = total + m_recv[k]
    m_cols[pl.ds(y, 1)] = total[None]

    def mx_out(k):
        return remote(m_cols.at[y], m_cols.at[y], mxs_sem.at[k], mxr_sem.at[y], i, image_of(k))

    def image_of(k):
        return 8 * xh + 2 * ((y + k) % 4) + core

    each(1, 4, lambda k: mx_out(k).start())
    pl.semaphore_wait(in_sem, 15)

    def mx_in(k):
        src = (y + 4 - k) % 4
        remote(m_cols.at[src], m_cols.at[src], mxs_sem.at[k], mxr_sem.at[src], i, sibling).wait_recv()

    each(1, 4, mx_in)
    total = jnp.zeros((72, 128), F32)
    for q in range(4):
        total = total + jnp.dot(m_cols[q], g_inv_ref[128 * q:128 * q + 128, here_y],
                                precision=lax.Precision.HIGHEST, preferred_element_type=F32)
    m_piece[...] = total
    m_to = 4 * a + i // 4

    def m_spot(rho, chunk):
        return m_rows.at[pl.ds(pl.multiple_of(72 * rho, 8), 72),
                         pl.ds(pl.multiple_of(128 * chunk, 128), 128)]

    m_here = 2 * (i % 4) + b % 2

    def mg_out(n):
        return remote(m_piece, m_spot(i % 4, b % 2), mgs_sem.at[n], mgr_sem.at[m_here], 8 * (b // 2) + n, m_to)

    def mg_mine(n):
        return (8 * (b // 2) + n == i) & (m_to == j)

    def mg_start(k):
        n = (z + k) % 8

        @pl.when(jnp.logical_not(mg_mine(n)))
        def _():
            mg_out(n).start()

        @pl.when(mg_mine(n))
        def _():
            pltpu.make_async_copy(m_piece, m_spot(i % 4, b % 2), mgr_sem.at[m_here]).start()

    each(0, 8, mg_start)

    def g_in(k):
        src = (j + 16 - k) % 16
        here = g_recv.at[src]
        remote(here, here, gs_sem.at[k], gr_sem.at[src], i, src).wait_recv()

    each(1, 16, g_in)
    total = g_recv[0].astype(F32)
    for k in range(1, 16):
        total = total + g_recv[k].astype(F32)
    g_sum[...] = total

    def g_spot(ref, who):
        return ref.at[pl.ds(pl.multiple_of(8 * (who // 4), 8), 8),
                      pl.ds(pl.multiple_of(128 * (who % 4), 128), 128)]

    def g2_out(k):
        to = (i + k) % 16
        return remote(g_spot(g_sum, to), g2_recv.at[i], g2s_sem.at[k], g2r_sem.at[i], to, j)

    each(1, 16, lambda k: g2_out(k).start())
    g2_recv[pl.ds(i, 1)] = g_sum[pl.ds(pl.multiple_of(8 * (i // 4), 8), 8),
                                 pl.ds(pl.multiple_of(128 * (i % 4), 128), 128)][None]

    @pl.when(i < 15)
    def _():
        def a_in(k):
            src = (i + 16 - k) % 16
            here = a_recv.at[src]
            remote(here, here, as_sem.at[0], ar_sem.at[src], src, j).wait_recv()

        each(1, 16, a_in)
        for half in range(2):
            span = slice(128 * half, 128 * half + 128)
            total = a_recv[0, span].astype(F32)
            for k in range(1, 16):
                total = total + a_recv[k, span].astype(F32)
            a_sum[2 * half] = total
            a_sum[2 * half + 1] = total.T

    def spread(act):
        def one(n):
            half = n // 32
            turned = (n // 16) % 2
            yp, xp, tj, ti = (n // 8) % 2, (n // 4) % 2, (n // 2) % 2, n % 2
            k = 2 * i + half
            flat = k < 15
            ey = jnp.where(flat, 0, jnp.where(k < 22, 1, 2))
            s = jnp.where(flat, k % 5, (k + 6) % 7)
            ex = jnp.where(s < 3, 0, jnp.where(s < 5, s - 2, 4 - s))
            row_y = jnp.where(flat, k // 5, yp)
            row_x = jnp.where(s < 3, s, jnp.where(s < 5, 0, s - 4)) + xp
            ok = (k < BLOCKS) & ((yp == 0) | (ey == 1)) & ((xp == 0) | (ex == 1) | (ex == -1))
            ok = ok & ((turned == 0) | (ey != 0) | (ex != 0))
            first = 4 * (3 * row_y + row_x) + a
            second = 4 * (3 * (row_y + ey) + row_x + ex) + b
            r = jnp.where(turned == 0, first, second)
            c = jnp.where(turned == 0, second, first)
            to_j = (4 * r) // 9 + tj
            to_i = (4 * c) // 9 + ti
            ok = ok & (to_j <= (128 * r + 127) // 288) & (to_i <= (128 * c + 127) // 288)
            at_r = r - (9 * to_j) // 4
            at_c = c - (9 * to_i) // 4
            src = a_sum.at[2 * half + turned]
            dst = tile.at[pl.ds(pl.multiple_of(128 * at_r, 128), 128),
                          pl.ds(pl.multiple_of(128 * at_c, 128), 128)]
            mine = (to_i == i) & (to_j == j)
            arrived = tr_sem.at[3 * at_r + at_c]

            @pl.when(ok & jnp.logical_not(mine))
            def _():
                act(remote(src, dst, ts_sem.at[n], arrived, to_i, to_j))

            if act is start:
                @pl.when(ok & mine)
                def _():
                    pltpu.make_async_copy(src, dst, arrived).start()

        each(0, 64, one)

    def start(copy):
        copy.start()

    def sent_off(copy):
        copy.wait_send()

    spread(start)

    for q in range(8):
        here = m_spot(q // 2, q % 2)
        remote(here, here, mgs_sem.at[0], mgr_sem.at[q], i, sibling).wait_recv()
    inv_out.wait_recv()
    lane = lax.broadcasted_iota(jnp.int32, (72, 128), 1) // 32
    for t in range(2):
        prod = jnp.dot(inv_both[t], m_rows[...], precision=lax.Precision.HIGHEST,
                       preferred_element_type=F32)
        for to in range(8):
            piece = jnp.zeros((72, 128), F32)
            for q in range(4):
                block = prod[72 * q:72 * q + 72, 128 * (to // 4):128 * (to // 4) + 128]
                shift = (32 * (q - to % 4)) % 128
                if shift:
                    block = pltpu.roll(block, shift, 1)
                piece = jnp.where(lane == q, block, piece)
            n_send[8 * t + to] = piece
    def n_out(n):
        return remote(n_send.at[n], n_recv.at[j], ns_sem.at[n], nr_sem.at[j], 8 * (n // 8) + z, 8 * xl + n % 8)

    def n_mine(n):
        return (n // 8 == xl) & (8 * xl + n % 8 == j)

    def n_start(k):
        n = (k + j) % 16

        @pl.when(jnp.logical_not(n_mine(n)))
        def _():
            n_out(n).start()

    each(0, 16, n_start)

    @pl.when(xl == j // 8)
    def _():
        n_recv[pl.ds(j, 1)] = n_send[pl.ds(j, 1)]

    def g2_in(k):
        src = (i + 16 - k) % 16
        here = g2_recv.at[src]
        remote(here, here, g2s_sem.at[k], g2r_sem.at[src], src, j).wait_recv()

    each(1, 16, g2_in)
    total = g2_recv[0]
    for k in range(1, 16):
        total = total + g2_recv[k]
    g_piece[...] = total

    def g3_out(k):
        return remote(g_piece, g_spot(g_fin, i), g3s_sem.at[k], g3r_sem.at[i], (i + k) % 16, j)

    each(1, 16, lambda k: g3_out(k).start())
    g_fin[pl.ds(pl.multiple_of(8 * (i // 4), 8), 8),
          pl.ds(pl.multiple_of(128 * (i % 4), 128), 128)] = total

    def c_in(k):
        q = (y + 4 - k) % 4
        here = c_recv.at[:, pl.ds(pl.multiple_of(128 * q, 128), 128)]
        remote(here, here, cs_sem.at[k], cr_sem.at[q], i, sibling).wait_recv()

    each(1, 4, c_in)
    conv_ref[...] = c_recv[...]

    for q in range(9):
        here = tile.at[pl.ds(128 * (q // 3), 128), pl.ds(128 * (q % 3), 128)]
        remote(here, here, ts_sem.at[0], tr_sem.at[q], i, sibling).wait_recv()
    rows = tile[pl.ds(pl.multiple_of(32 * (j % 4), 32), 288), :]
    rows = pltpu.roll(rows, (384 - 32 * (i % 4)) % 384, 1)[:, 0:288]
    a_ref[...] = 0.5 * a_old_ref[...] + (0.5 / 65536.0) * rows

    def g3_in(k):
        src = (i + 16 - k) % 16
        here = g_spot(g_fin, src)
        remote(here, here, g3s_sem.at[k], g3r_sem.at[src], src, j).wait_recv()

    each(1, 16, g3_in)
    g_ref[...] = 0.5 * g_old_ref[...] + 0.5 * g_fin[...]

    def n_in(src):
        @pl.when(jnp.logical_not((src == j) & (xl == j // 8)))
        def _():
            here = n_recv.at[src]
            remote(here, here, ns_sem.at[0], nr_sem.at[src], i, sibling).wait_recv()

    each(0, 16, n_in)
    total = n_recv[0]
    for k in range(1, 16):
        total = total + n_recv[k]
    ng_ref[...] = total

    for n in range(4):
        x_own(n).wait_send()
    for n in range(2):
        x_pass(n).wait_send()
        x_half(0, n).wait_send()
        x_half(1, n).wait_send()
    inv_out.wait_send()
    z_sib.wait_send()
    each(1, 8, lambda k: z_out(k).wait_send())

    def handed(k):
        who = (j + 2 * k) % 16
        x_fwd(who).wait_send()
        z_fwd(who).wait_send()

    each(1, 8, handed)
    w_each(lambda k: w_out(k).wait_send())
    w_each(lambda k: w_fwd(k).wait_send())
    each(1, 4, lambda k: mx_out(k).wait_send())
    each(1, 4, lambda k: c_out(k).wait_send())

    def rest_sent(k):
        g_out(k).wait_send()
        m_out(k).wait_send()
        g2_out(k).wait_send()
        g3_out(k).wait_send()

    each(1, 16, rest_sent)

    def a_sent(to):
        @pl.when(to != i)
        def _():
            a_out(to).wait_send()

    each(0, 15, a_sent)

    def mg_sent(n):
        @pl.when(jnp.logical_not(mg_mine(n)))
        def _():
            mg_out(n).wait_send()

    each(0, 8, mg_sent)

    def n_sent(n):
        @pl.when(jnp.logical_not(n_mine(n)))
        def _():
            n_out(n).wait_send()

    each(0, 16, n_sent)
    spread(sent_off)


def per_device(activations, cotangent, weight, a_factor_old, g_factor_old, a_inverse, g_inverse):
    vmem = pl.BlockSpec(memory_space=pltpu.VMEM)
    dma = pltpu.SemaphoreType.DMA
    conv, a_factor, g_factor, packed = pl.pallas_call(
        kernel,
        name="kfac_step",
        out_shape=(
            jax.ShapeDtypeStruct((256, 512), BF16),
            jax.ShapeDtypeStruct((288, 288), F32),
            jax.ShapeDtypeStruct((32, 512), F32),
            jax.ShapeDtypeStruct((72, 128), F32),
        ),
        in_specs=[vmem] * 7,
        out_specs=(vmem,) * 4,
        scratch_shapes=[
            pltpu.VMEM((16, 288, 512), BF16),
            pltpu.VMEM((512, 256), BF16),
            pltpu.VMEM((384, 256), BF16),
            pltpu.VMEM((288, 384), BF16),
            pltpu.VMEM((16, 256, 128), BF16),
            pltpu.VMEM((3, 288, 128), BF16),
            pltpu.VMEM((4608, 128), BF16),
            pltpu.VMEM((5, 384, 384), F32),
            pltpu.VMEM((2, 288, 288), F32),
            pltpu.VMEM((1152, 128), F32),
            pltpu.VMEM((16, 72, 128), F32),
            pltpu.VMEM((4, 72, 128), F32),
            pltpu.VMEM((72, 128), F32),
            pltpu.VMEM((288, 256), F32),
            pltpu.VMEM((16, 72, 128), F32),
            pltpu.VMEM((16, 72, 128), F32),
            pltpu.VMEM((3840, 128), BF16),
            pltpu.VMEM((16, 256, 128), BF16),
            pltpu.VMEM((4, 128, 128), F32),
            pltpu.VMEM((384, 384), F32),
            pltpu.VMEM((512, 512), BF16),
            pltpu.VMEM((16, 32, 512), BF16),
            pltpu.VMEM((32, 512), F32),
            pltpu.VMEM((16, 8, 128), F32),
            pltpu.VMEM((8, 128), F32),
            pltpu.VMEM((32, 512), F32),
            pltpu.VMEM((4, 256, 128), BF16),
            pltpu.VMEM((256, 512), BF16),
            pltpu.SemaphoreType.REGULAR,
            dma((2,)),
            dma((10,)), dma((16,)), dma((16,)), dma((16,)),
            dma((8,)), dma((16,)), dma((8,)),
            dma((16,)), dma((16,)), dma((16,)),
            dma((16,)), dma((16,)), dma((4,)), dma((4,)), dma((16,)), dma((16,)),
            dma((16,)), dma((16,)),
            dma((16,)), dma((16,)), dma((64,)), dma((9,)),
            dma((16,)), dma((16,)), dma((16,)), dma((16,)), dma((16,)), dma((16,)),
            dma((4,)), dma((4,)),
        ],
        compiler_params=pltpu.CompilerParams(
            collective_id=0, has_side_effects=True, vmem_limit_bytes=56 * 1024 * 1024),
        cost_estimate=pl.CostEstimate(flops=15_000_000_000, bytes_accessed=4_000_000, transcendentals=0),
    )(activations.reshape(256, 512), cotangent.reshape(256, 512), weight, a_factor_old, g_factor_old, a_inverse, g_inverse)
    natural = packed.reshape(72, 4, 32).transpose(1, 0, 2).reshape(288, 32).astype(BF16)
    return conv.reshape(1, 16, 16, 512), a_factor, g_factor, natural


def solution(mesh):
    return jax.shard_map(
        per_device,
        mesh=mesh,
        in_specs=(
            P(("fsdp", "factor"), None, None, None),
            P(("fsdp", "factor"), None, None, None),
            P("fsdp", None),
            P("factor", "fsdp"),
            P("factor", None),
            P("fsdp", "factor"),
            P(),
        ),
        out_specs=(
            P(("fsdp", "factor"), None, None, None),
            P("factor", "fsdp"),
            P("factor", None),
            P("fsdp", "factor"),
        ),
        check_vma=False,
    )
```

```python
import jax
import jax.numpy as jnp
from jax import lax
from jax.experimental import pallas as pl
from jax.experimental.pallas import tpu as pltpu
from jax.sharding import PartitionSpec as P

MESH = pl.DeviceIdType.MESH
F32 = jnp.float32
BF16 = jnp.bfloat16
X_BLOCKS = ((0, 0), (1, 1), (2, 2), (0, 1), (0, 2), (1, 0), (2, 0))
COUNTS = (5, 5, 5, 7, 7)
SLOTS = (
    1, 22, 15, 25, 4, 21, 20, 2, 23, 11, 28, 14, 5, 17, 8, 13,
    19, 12, 3, 9, 10, 18, 16, 27, -1, -1, -1, 6, 26, 24, 0, 7,
)
IDLE = 12


def kernel(
    x_ref, dy_ref, w_ref, a_inv_ref, g_inv_ref,
    conv_ref, a_ref, g_ref, ng_ref,
    x_all, x_t, xa_t, xb, z_all, z_sh, w_all, a_acc, inv_both,
    m_part, m_recv, m_cols, m_piece, m_rows, n_send, n_recv,
    a_send, a_recv, a_sum, tile, g_send, g_recv, g_sum, g2_recv, g_piece, g_fin,
    c_send, c_recv,
    in_sem, inv_sem, xs_sem, xr_sem, xh_sem, xf_sem, zs_sem, zr_sem, zf_sem, ws_sem, wr_sem, wf_sem,
    ms_sem, mr_sem, mxs_sem, mxr_sem, mgs_sem, mgr_sem, ns_sem, nr_sem, as_sem, ar_sem, ts_sem, tr_sem,
    gs_sem, gr_sem, g2s_sem, g2r_sem, g3s_sem, g3r_sem, cs_sem, cr_sem,
):
    i = lax.axis_index("fsdp")
    j = lax.axis_index("factor")
    xh, y, core = j // 8, (j // 2) % 4, j % 2
    a = 2 * xh + core
    b = y
    sibling = j + 1 - 2 * core
    xl, z = i // 8, i % 8

    def remote(src, dst, send, recv, dev_i, dev_j):
        return pltpu.make_async_remote_copy(
            src_ref=src, dst_ref=dst, send_sem=send, recv_sem=recv,
            device_id=(dev_i, dev_j), device_id_type=MESH,
        )

    def each(lo, hi, body):
        def step(k, carry):
            body(k)
            return carry
        lax.fori_loop(lo, hi, step, 0)

    entry = pltpu.get_barrier_semaphore()

    def greet(k):
        pl.semaphore_signal(entry, inc=1, device_id=((i + k) % 16, j), device_id_type=MESH)
        pl.semaphore_signal(entry, inc=1, device_id=(i, (j + k) % 16), device_id_type=MESH)

    each(1, 16, greet)
    pl.semaphore_wait(entry, 30)
    each(1, 16, lambda k: pl.semaphore_signal(
        in_sem, inc=1, device_id=(i, (j + k) % 16), device_id_type=MESH))

    def image(half, step):
        return 8 * ((xh + half) % 2) + 2 * ((y + step + 4) % 4) + core

    def x_at(who, lo=0, size=256):
        return x_all.at[who, pl.ds(16 + lo, size)]

    def x_own(n):
        to = (image(0, 1), image(0, -1), image(1, 0), sibling)[n]
        return remote(x_ref, x_at(j), xs_sem.at[n], xr_sem.at[j], i, to)

    def x_pass(n):
        who = image(1, 0)
        return remote(x_at(who), x_at(who), xs_sem.at[4 + n], xr_sem.at[who], i, image(0, 1 - 2 * n))

    def x_half(half, n):
        step = 1 - 2 * n
        who = image(half, -step)
        here = x_at(who, 128 * n, 128)
        return remote(here, here, xs_sem.at[6 + 2 * half + n], (xr_sem, xh_sem)[n].at[who], i, image(0, step))

    def x_fwd(who):
        return remote(x_at(who), x_at(who), xf_sem.at[who], xr_sem.at[who], i, sibling)

    def x_got(who, lo=0, size=256, sem=None):
        here = x_at(who, lo, size)
        remote(here, here, xf_sem.at[who], (xr_sem if sem is None else sem).at[who], i, sibling).wait_recv()

    for n in range(4):
        x_own(n).start()

    def z_out(k):
        to = (j + 2 * k) % 16
        return remote(dy_ref.at[:, pl.ds(pl.multiple_of(128 * ((to // 2) % 4), 128), 128)],
                      z_all.at[j], zs_sem.at[k], zr_sem.at[j], i, to)

    each(1, 8, lambda k: z_out(k).start())
    here_y = pl.ds(pl.multiple_of(128 * y, 128), 128)
    z_sib = remote(dy_ref.at[:, here_y], z_all.at[j], zs_sem.at[0], zr_sem.at[j], i, sibling)
    z_sib.start()

    def w_at(who):
        return w_all.at[pl.ds(pl.multiple_of(288 * who, 32), 288)]

    def w_out(k):
        return remote(w_ref.at[:, here_y], w_at(i), ws_sem.at[k], wr_sem.at[i], (i + k) % 16, j)

    w_lo = 2 - core

    def w_each(body):
        def step(n, carry):
            body(2 * n + w_lo)
            return carry
        lax.fori_loop(0, 7 + core, step, 0)

    inv_out = remote(a_inv_ref, inv_both.at[xl], inv_sem.at[0], inv_sem.at[1], (i + 8) % 16, j)

    def clear(who):
        x_all[pl.ds(who, 1), 0:16] = jnp.zeros((1, 16, 512), BF16)
        x_all[pl.ds(who, 1), 272:288] = jnp.zeros((1, 16, 512), BF16)

    each(0, 16, clear)
    x_all[pl.ds(j, 1), 16:272] = x_ref[...][None]
    z_all[pl.ds(j, 1)] = dy_ref[:, here_y][None]
    w_all[pl.ds(pl.multiple_of(288 * i, 32), 288), :] = w_ref[:, here_y]
    inv_both[pl.ds(xl, 1)] = a_inv_ref[...][None]
    xb[256:288, :] = jnp.zeros((32, 384), BF16)
    for dx in range(3):
        z_sh[dx, 0:16] = jnp.zeros((16, 128), BF16)
        z_sh[dx, 272:288] = jnp.zeros((16, 128), BF16)
    a_acc[...] = jnp.zeros((5, 384, 384), F32)
    m_part[...] = jnp.zeros((1152, 128), F32)

    col = lax.broadcasted_iota(jnp.int32, (128, 256), 1) % 16
    row = lax.broadcasted_iota(jnp.int32, (256, 128), 0) % 16
    map_row = lax.broadcasted_iota(jnp.int32, (256, 384), 0) // 16
    none = jnp.zeros((256, 384), BF16)

    def terms(who):
        x_t[...] = x_all[pl.ds(who, 1), 16:272].reshape(256, 512).T
        mid = x_t[pl.ds(pl.multiple_of(128 * a, 128), 128), :]
        wide = mid.astype(F32)
        xa_t[0:128] = jnp.where(col == 0, 0.0, pltpu.roll(wide, 1, 1)).astype(BF16)
        xa_t[128:256] = mid
        xa_t[256:384] = jnp.where(col == 15, 0.0, pltpu.roll(wide, 255, 1)).astype(BF16)
        mid = x_all[pl.ds(who, 1), 16:272, here_y].reshape(256, 128)
        wide = mid.astype(F32)
        xb[0:256, 0:128] = jnp.where(row == 0, 0.0, pltpu.roll(wide, 1, 0)).astype(BF16)
        xb[0:256, 128:256] = mid
        xb[0:256, 256:384] = jnp.where(row == 15, 0.0, pltpu.roll(wide, 255, 0)).astype(BF16)
        mid = z_all[pl.ds(who, 1)].reshape(256, 128)
        wide = mid.astype(F32)
        z_sh[0, 16:272] = jnp.where(row == 15, 0.0, pltpu.roll(wide, 255, 0)).astype(BF16)
        z_sh[1, 16:272] = mid
        z_sh[2, 16:272] = jnp.where(row == 0, 0.0, pltpu.roll(wide, 1, 0)).astype(BF16)
        lhs = xa_t[...]
        flat = xb[0:256, :]
        a_acc[0] += jnp.dot(lhs, jnp.where(map_row == 15, none, flat), preferred_element_type=F32)
        a_acc[1] += jnp.dot(lhs, flat, preferred_element_type=F32)
        a_acc[2] += jnp.dot(lhs, jnp.where(map_row == 0, none, flat), preferred_element_type=F32)
        a_acc[3] += jnp.dot(lhs, xb[16:272, :], preferred_element_type=F32)
        a_acc[4] += jnp.dot(lhs, xb[32:288, :], preferred_element_type=F32)
        for k in range(9):
            r = 9 * a + k
            tap = r // 4
            part = jnp.dot(x_t[pl.ds(pl.multiple_of(128 * (r % 4), 128), 128), :],
                           z_sh[tap % 3, pl.ds(pl.multiple_of(32 - 16 * (tap // 3), 16), 256), :],
                           preferred_element_type=F32)
            m_part[128 * k:128 * k + 128, :] += part

    def z_fwd(who):
        return remote(z_all.at[who], z_all.at[who], zf_sem.at[who // 2], zr_sem.at[who], i, sibling)

    def z_got(who):
        remote(z_all.at[who], z_all.at[who], zf_sem.at[0], zr_sem.at[who], i, sibling).wait_recv()

    def hand_on(who):
        x_fwd(who).start()
        z_got(who)
        z_fwd(who).start()

    def from_ring(half, n):
        x_got(image(half, 2 * n - 1))
        x_half(half, n).start()
        hand_on(image(half, 2 * n - 1))

    def from_far(half):
        who = image(half, 2)
        x_got(who, 0, 128)
        x_got(who, 128, 128, xh_sem)
        hand_on(who)

    def arrivals(n, carry):
        @pl.when(n == 1)
        def _():
            from_ring(0, 0)
            from_ring(0, 1)
            x_got(image(1, 0))
            x_pass(0).start()
            x_pass(1).start()
            hand_on(image(1, 0))
            w_each(lambda k: w_out(k).start())

        @pl.when(n == 3)
        def _():
            from_far(0)

        @pl.when(n == 5)
        def _():
            from_ring(1, 0)
            from_ring(1, 1)

        @pl.when(n == 7)
        def _():
            from_far(1)

        half = jnp.where((n == 3) | (n > 4), 1, 0)
        step = jnp.where((n == 0) | (n == 3), 0, jnp.where((n == 1) | (n == 5), 3, jnp.where((n == 2) | (n == 6), 1, 2)))
        mine = image(half, step)

        def one(c, carry):
            who = jnp.where(c == 0, mine, mine + 1 - 2 * core)

            @pl.when(c == 1)
            def _():
                x_got(who)
                z_got(who)

            terms(who)
            return carry

        return lax.fori_loop(0, 2, one, carry)

    lax.fori_loop(0, 8, arrivals, 0)

    def w_in(k):
        src = (i + 16 - k) % 16
        remote(w_at(src), w_at(src), ws_sem.at[k], wr_sem.at[src], src, j).wait_recv()

    def w_fwd(k):
        src = (i + 16 - k) % 16
        return remote(w_at(src), w_at(src), wf_sem.at[k], wr_sem.at[src], i, sibling)

    def w_forward(k):
        w_in(k)
        w_fwd(k).start()

    def m_out(k):
        to = (i + k) % 16
        return remote(m_part.at[pl.ds(pl.multiple_of(72 * to, 8), 72)], m_recv.at[i],
                      ms_sem.at[k], mr_sem.at[i], to, j)

    each(1, 16, lambda k: m_out(k).start())
    inv_out.start()
    m_recv[pl.ds(i, 1)] = m_part[pl.ds(pl.multiple_of(72 * i, 8), 72)][None]

    cot = dy_ref[...]
    g_send[...] = lax.dot_general(
        cot, cot, (((0,), (0,)), ((), ())), preferred_element_type=F32).astype(BF16)

    def g_out(k):
        to = (j + k) % 16
        return remote(g_send.at[pl.ds(pl.multiple_of(32 * to, 32), 32)], g_recv.at[j],
                      gs_sem.at[k], gr_sem.at[j], i, to)

    each(1, 16, lambda k: g_out(k).start())
    g_recv[pl.ds(j, 1)] = g_send[pl.ds(pl.multiple_of(32 * j, 32), 32)][None]

    own_slot = (i + 11 * j) % 16

    def a_to(slot):
        return (slot + 5 * j) % 16

    def a_out(slot):
        return remote(a_send.at[pl.ds(pl.multiple_of(256 * slot, 256), 256)], a_recv.at[i],
                      as_sem.at[slot], ar_sem.at[i], a_to(slot), j)

    def a_start(k):
        slot = (own_slot + k) % 16

        @pl.when(slot != IDLE)
        def _():
            a_out(slot).start()

    at_block = 0
    for combo, count in enumerate(COUNTS):
        part = a_acc[combo]
        for row_x, col_x in X_BLOCKS[:count]:
            spot = 128 * SLOTS.index(at_block)
            a_send[spot:spot + 128, :] = part[
                128 * row_x:128 * row_x + 128, 128 * col_x:128 * col_x + 128].astype(BF16)
            at_block += 1
    for spot, block in enumerate(SLOTS):
        if block < 0:
            a_send[128 * spot:128 * spot + 128, :] = jnp.zeros((128, 128), BF16)
    each(1, 16, a_start)

    @pl.when(own_slot != IDLE)
    def _():
        a_recv[pl.ds(i, 1)] = a_send[pl.ds(pl.multiple_of(256 * own_slot, 256), 256)][None]

    w_each(w_forward)

    def w_other(k):
        @pl.when(k % 2 != core)
        def _():
            w_in(k)

    each(1, 16, w_other)
    conv_row = lax.broadcasted_iota(jnp.int32, (256, 128), 0) % 16

    def conv_image(q):
        who = 8 * xh + 2 * q + core
        parts = []
        for dx in range(3):
            total = jnp.zeros((256, 128), F32)
            for dy in range(3):
                total = total + jnp.dot(
                    x_all[pl.ds(who, 1), 16 * dy:16 * dy + 256].reshape(256, 512),
                    w_all[512 * (3 * dy + dx):512 * (3 * dy + dx) + 512, :],
                    preferred_element_type=F32)
            parts.append(total)
        out = parts[1] + jnp.where(conv_row == 0, 0.0, pltpu.roll(parts[0], 1, 0))
        out = out + jnp.where(conv_row == 15, 0.0, pltpu.roll(parts[2], 255, 0))
        c_send[pl.ds(q, 1)] = out.astype(BF16)[None]

    each(0, 4, conv_image)

    def c_out(k):
        q = (y + k) % 4
        return remote(c_send.at[q], c_recv.at[:, here_y], cs_sem.at[k], cr_sem.at[y],
                      i, 8 * xh + 2 * q + core)

    each(1, 4, lambda k: c_out(k).start())
    c_recv[:, here_y] = c_send[y]

    def m_in(k):
        src = (i + 16 - k) % 16
        here = m_recv.at[src]
        remote(here, here, ms_sem.at[k], mr_sem.at[src], src, j).wait_recv()

    each(1, 16, m_in)
    total = m_recv[0]
    for k in range(1, 16):
        total = total + m_recv[k]
    m_cols[pl.ds(y, 1)] = total[None]

    def mx_out(k):
        return remote(m_cols.at[y], m_cols.at[y], mxs_sem.at[k], mxr_sem.at[y], i, image_of(k))

    def image_of(k):
        return 8 * xh + 2 * ((y + k) % 4) + core

    each(1, 4, lambda k: mx_out(k).start())
    pl.semaphore_wait(in_sem, 15)

    def mx_in(k):
        src = (y + 4 - k) % 4
        remote(m_cols.at[src], m_cols.at[src], mxs_sem.at[k], mxr_sem.at[src], i, sibling).wait_recv()

    each(1, 4, mx_in)
    total = jnp.zeros((72, 128), F32)
    for q in range(4):
        total = total + jnp.dot(m_cols[q], g_inv_ref[128 * q:128 * q + 128, here_y],
                                precision=lax.Precision.HIGHEST, preferred_element_type=F32)
    m_piece[...] = total
    m_to = 4 * a + i // 4

    def m_spot(rho, chunk):
        return m_rows.at[pl.ds(pl.multiple_of(72 * rho, 8), 72),
                         pl.ds(pl.multiple_of(128 * chunk, 128), 128)]

    m_here = 2 * (i % 4) + b % 2

    def mg_out(n):
        return remote(m_piece, m_spot(i % 4, b % 2), mgs_sem.at[n], mgr_sem.at[m_here], 8 * (b // 2) + n, m_to)

    def mg_mine(n):
        return (8 * (b // 2) + n == i) & (m_to == j)

    def mg_start(k):
        n = (z + k) % 8

        @pl.when(jnp.logical_not(mg_mine(n)))
        def _():
            mg_out(n).start()

        @pl.when(mg_mine(n))
        def _():
            pltpu.make_async_copy(m_piece, m_spot(i % 4, b % 2), mgr_sem.at[m_here]).start()

    each(0, 8, mg_start)

    def g_in(k):
        src = (j + 16 - k) % 16
        here = g_recv.at[src]
        remote(here, here, gs_sem.at[k], gr_sem.at[src], i, src).wait_recv()

    each(1, 16, g_in)
    total = g_recv[0].astype(F32)
    for k in range(1, 16):
        total = total + g_recv[k].astype(F32)
    g_sum[...] = total

    def g_spot(ref, who):
        return ref.at[pl.ds(pl.multiple_of(8 * (who // 4), 8), 8),
                      pl.ds(pl.multiple_of(128 * (who % 4), 128), 128)]

    def g2_out(k):
        to = (i + k) % 16
        return remote(g_spot(g_sum, to), g2_recv.at[i], g2s_sem.at[k], g2r_sem.at[i], to, j)

    each(1, 16, lambda k: g2_out(k).start())
    g2_recv[pl.ds(i, 1)] = g_sum[pl.ds(pl.multiple_of(8 * (i // 4), 8), 8),
                                 pl.ds(pl.multiple_of(128 * (i % 4), 128), 128)][None]

    @pl.when(own_slot != IDLE)
    def _():
        def a_in(k):
            src = (i + 16 - k) % 16
            here = a_recv.at[src]
            remote(here, here, as_sem.at[0], ar_sem.at[src], src, j).wait_recv()

        each(1, 16, a_in)
        for half in range(2):
            span = slice(128 * half, 128 * half + 128)
            total = a_recv[0, span].astype(F32)
            for k in range(1, 16):
                total = total + a_recv[k, span].astype(F32)
            a_sum[2 * half] = total
            a_sum[2 * half + 1] = total.T

    def block_in(slot):
        block = jnp.int32(-1)
        for spot, held in enumerate(SLOTS):
            block = jnp.where(slot == spot, held, block)
        return block

    def spread(act):
        for half in range(2):
            k = block_in(2 * own_slot + half)
            flat = k < 15
            ey = jnp.where(flat, 0, jnp.where(k < 22, 1, 2))
            s = jnp.where(flat, (k + 5) % 5, (k + 6) % 7)
            ex = jnp.where(s < 3, 0, jnp.where(s < 5, s - 2, 4 - s))
            low_x = jnp.where(s < 3, s, jnp.where(s < 5, 0, s - 4))
            low_y = jnp.where(flat, (k + 5) // 5 - 1, 0)

            def place(n):
                turned, yp, xp = n // 4, (n // 2) % 2, n % 2
                ok = (k >= 0) & ((yp == 0) | (ey == 1)) & ((xp == 0) | (ex == 1) | (ex == -1))
                ok = ok & ((turned == 0) | (ey != 0) | (ex != 0))

                @pl.when(ok)
                def _():
                    row_y, row_x = low_y + yp, low_x + xp
                    first = 4 * (3 * row_y + row_x) + a
                    second = 4 * (3 * (row_y + ey) + row_x + ex) + b
                    r = jnp.where(turned == 0, first, second)
                    c = jnp.where(turned == 0, second, first)
                    src = a_sum.at[2 * half + turned]
                    for t in range(4):
                        to_j = (4 * r) // 9 + t // 2
                        to_i = (4 * c) // 9 + t % 2
                        inside = (to_j <= (128 * r + 127) // 288) & (to_i <= (128 * c + 127) // 288)
                        at_r = r - (9 * to_j) // 4
                        at_c = c - (9 * to_i) // 4
                        mine = (to_i == i) & (to_j == j)

                        @pl.when(inside)
                        def _():
                            dst = tile.at[pl.ds(pl.multiple_of(128 * at_r, 128), 128),
                                          pl.ds(pl.multiple_of(128 * at_c, 128), 128)]
                            arrived = tr_sem.at[3 * at_r + at_c]

                            @pl.when(jnp.logical_not(mine))
                            def _():
                                act(remote(src, dst, ts_sem.at[32 * half + 4 * n + t], arrived, to_i, to_j))

                            if act is start:
                                @pl.when(mine)
                                def _():
                                    pltpu.make_async_copy(src, dst, arrived).start()

            each(0, 8, place)

    def start(copy):
        copy.start()

    def sent_off(copy):
        copy.wait_send()

    spread(start)

    for q in range(8):
        here = m_spot(q // 2, q % 2)
        remote(here, here, mgs_sem.at[0], mgr_sem.at[q], i, sibling).wait_recv()
    inv_out.wait_recv()
    lane = lax.broadcasted_iota(jnp.int32, (72, 128), 1) // 32
    for t in range(2):
        prod = jnp.dot(inv_both[t], m_rows[...], precision=lax.Precision.HIGHEST,
                       preferred_element_type=F32)
        for to in range(8):
            piece = jnp.zeros((72, 128), F32)
            for q in range(4):
                block = prod[72 * q:72 * q + 72, 128 * (to // 4):128 * (to // 4) + 128]
                shift = (32 * (q - to % 4)) % 128
                if shift:
                    block = pltpu.roll(block, shift, 1)
                piece = jnp.where(lane == q, block, piece)
            n_send[8 * t + to] = piece
    def n_out(n):
        return remote(n_send.at[n], n_recv.at[j], ns_sem.at[n], nr_sem.at[j], 8 * (n // 8) + z, 8 * xl + n % 8)

    def n_mine(n):
        return (n // 8 == xl) & (8 * xl + n % 8 == j)

    def n_start(k):
        n = (k + j) % 16

        @pl.when(jnp.logical_not(n_mine(n)))
        def _():
            n_out(n).start()

    each(0, 16, n_start)

    @pl.when(xl == j // 8)
    def _():
        n_recv[pl.ds(j, 1)] = n_send[pl.ds(j, 1)]

    def g2_in(k):
        src = (i + 16 - k) % 16
        here = g2_recv.at[src]
        remote(here, here, g2s_sem.at[k], g2r_sem.at[src], src, j).wait_recv()

    each(1, 16, g2_in)
    total = g2_recv[0]
    for k in range(1, 16):
        total = total + g2_recv[k]
    g_piece[...] = total

    def g3_out(k):
        return remote(g_piece, g_spot(g_fin, i), g3s_sem.at[k], g3r_sem.at[i], (i + k) % 16, j)

    each(1, 16, lambda k: g3_out(k).start())
    g_fin[pl.ds(pl.multiple_of(8 * (i // 4), 8), 8),
          pl.ds(pl.multiple_of(128 * (i % 4), 128), 128)] = total

    def c_in(k):
        q = (y + 4 - k) % 4
        here = c_recv.at[:, pl.ds(pl.multiple_of(128 * q, 128), 128)]
        remote(here, here, cs_sem.at[k], cr_sem.at[q], i, sibling).wait_recv()

    each(1, 4, c_in)
    conv_ref[...] = c_recv[...]

    for q in range(9):
        here = tile.at[pl.ds(128 * (q // 3), 128), pl.ds(128 * (q % 3), 128)]
        remote(here, here, ts_sem.at[0], tr_sem.at[q], i, sibling).wait_recv()
    rows = tile[pl.ds(pl.multiple_of(32 * (j % 4), 32), 288), :]
    rows = pltpu.roll(rows, (384 - 32 * (i % 4)) % 384, 1)[:, 0:288]
    a_ref[...] = rows

    def g3_in(k):
        src = (i + 16 - k) % 16
        here = g_spot(g_fin, src)
        remote(here, here, g3s_sem.at[k], g3r_sem.at[src], src, j).wait_recv()

    each(1, 16, g3_in)
    g_ref[...] = g_fin[...]

    def n_in(src):
        @pl.when(jnp.logical_not((src == j) & (xl == j // 8)))
        def _():
            here = n_recv.at[src]
            remote(here, here, ns_sem.at[0], nr_sem.at[src], i, sibling).wait_recv()

    each(0, 16, n_in)
    total = n_recv[0]
    for k in range(1, 16):
        total = total + n_recv[k]
    ng_ref[...] = total

    for n in range(4):
        x_own(n).wait_send()
    for n in range(2):
        x_pass(n).wait_send()
        x_half(0, n).wait_send()
        x_half(1, n).wait_send()
    inv_out.wait_send()
    z_sib.wait_send()
    each(1, 8, lambda k: z_out(k).wait_send())

    def handed(k):
        who = (j + 2 * k) % 16
        x_fwd(who).wait_send()
        z_fwd(who).wait_send()

    each(1, 8, handed)
    w_each(lambda k: w_out(k).wait_send())
    w_each(lambda k: w_fwd(k).wait_send())
    each(1, 4, lambda k: mx_out(k).wait_send())
    each(1, 4, lambda k: c_out(k).wait_send())

    def rest_sent(k):
        g_out(k).wait_send()
        m_out(k).wait_send()
        g2_out(k).wait_send()
        g3_out(k).wait_send()

    each(1, 16, rest_sent)

    def a_sent(slot):
        @pl.when((slot != IDLE) & (slot != own_slot))
        def _():
            a_out(slot).wait_send()

    each(0, 16, a_sent)

    def mg_sent(n):
        @pl.when(jnp.logical_not(mg_mine(n)))
        def _():
            mg_out(n).wait_send()

    each(0, 8, mg_sent)

    def n_sent(n):
        @pl.when(jnp.logical_not(n_mine(n)))
        def _():
            n_out(n).wait_send()

    each(0, 16, n_sent)
    spread(sent_off)


def finish(conv_ref, a_sum_ref, g_sum_ref, packed_ref, a_old_ref, g_old_ref, out_ref, a_ref, g_ref, ng_ref):
    out_ref[...] = conv_ref[...]
    a_ref[...] = 0.5 * a_old_ref[...] + (0.5 / 65536.0) * a_sum_ref[...]
    g_ref[...] = 0.5 * g_old_ref[...] + 0.5 * g_sum_ref[...]
    packed = packed_ref[...]
    rows = [packed[:, 0:32]] + [pltpu.roll(packed, 128 - 32 * q, 1)[:, 0:32] for q in range(1, 4)]
    ng_ref[...] = jnp.concatenate(rows, axis=0).T.astype(BF16)


def per_device(activations, cotangent, weight, a_factor_old, g_factor_old, a_inverse, g_inverse):
    vmem = pl.BlockSpec(memory_space=pltpu.VMEM)
    dma = pltpu.SemaphoreType.DMA
    conv, a_factor, g_factor, packed = pl.pallas_call(
        kernel,
        name="kfac_step",
        out_shape=(
            jax.ShapeDtypeStruct((256, 512), BF16),
            jax.ShapeDtypeStruct((288, 288), F32),
            jax.ShapeDtypeStruct((32, 512), F32),
            jax.ShapeDtypeStruct((72, 128), F32),
        ),
        in_specs=[vmem] * 5,
        out_specs=(vmem,) * 4,
        scratch_shapes=[
            pltpu.VMEM((16, 288, 512), BF16),
            pltpu.VMEM((512, 256), BF16),
            pltpu.VMEM((384, 256), BF16),
            pltpu.VMEM((288, 384), BF16),
            pltpu.VMEM((16, 256, 128), BF16),
            pltpu.VMEM((3, 288, 128), BF16),
            pltpu.VMEM((4608, 128), BF16),
            pltpu.VMEM((5, 384, 384), F32),
            pltpu.VMEM((2, 288, 288), F32),
            pltpu.VMEM((1152, 128), F32),
            pltpu.VMEM((16, 72, 128), F32),
            pltpu.VMEM((4, 72, 128), F32),
            pltpu.VMEM((72, 128), F32),
            pltpu.VMEM((288, 256), F32),
            pltpu.VMEM((16, 72, 128), F32),
            pltpu.VMEM((16, 72, 128), F32),
            pltpu.VMEM((4096, 128), BF16),
            pltpu.VMEM((16, 256, 128), BF16),
            pltpu.VMEM((4, 128, 128), F32),
            pltpu.VMEM((384, 384), F32),
            pltpu.VMEM((512, 512), BF16),
            pltpu.VMEM((16, 32, 512), BF16),
            pltpu.VMEM((32, 512), F32),
            pltpu.VMEM((16, 8, 128), F32),
            pltpu.VMEM((8, 128), F32),
            pltpu.VMEM((32, 512), F32),
            pltpu.VMEM((4, 256, 128), BF16),
            pltpu.VMEM((256, 512), BF16),
            pltpu.SemaphoreType.REGULAR,
            dma((2,)),
            dma((10,)), dma((16,)), dma((16,)), dma((16,)),
            dma((8,)), dma((16,)), dma((8,)),
            dma((16,)), dma((16,)), dma((16,)),
            dma((16,)), dma((16,)), dma((4,)), dma((4,)), dma((16,)), dma((16,)),
            dma((16,)), dma((16,)),
            dma((16,)), dma((16,)), dma((64,)), dma((9,)),
            dma((16,)), dma((16,)), dma((16,)), dma((16,)), dma((16,)), dma((16,)),
            dma((4,)), dma((4,)),
        ],
        compiler_params=pltpu.CompilerParams(
            collective_id=0, has_side_effects=True, vmem_limit_bytes=56 * 1024 * 1024),
        cost_estimate=pl.CostEstimate(flops=15_000_000_000, bytes_accessed=4_000_000, transcendentals=0),
    )(activations.reshape(256, 512), cotangent.reshape(256, 512), weight, a_inverse, g_inverse)
    conv, a_factor, g_factor, natural = pl.pallas_call(
        finish,
        name="finish",
        out_shape=(
            jax.ShapeDtypeStruct((256, 512), BF16),
            jax.ShapeDtypeStruct((288, 288), F32),
            jax.ShapeDtypeStruct((32, 512), F32),
            jax.ShapeDtypeStruct((32, 288), BF16),
        ),
        in_specs=[vmem] * 6,
        out_specs=(vmem,) * 4,
        cost_estimate=pl.CostEstimate(flops=1_000_000, bytes_accessed=2_000_000, transcendentals=0),
    )(conv, a_factor, g_factor, packed, a_factor_old, g_factor_old)
    return conv.reshape(1, 16, 16, 512), a_factor, g_factor, natural.T


def solution(mesh):
    return jax.shard_map(
        per_device,
        mesh=mesh,
        in_specs=(
            P(("fsdp", "factor"), None, None, None),
            P(("fsdp", "factor"), None, None, None),
            P("fsdp", None),
            P("factor", "fsdp"),
            P("factor", None),
            P("fsdp", "factor"),
            P(),
        ),
        out_specs=(
            P(("fsdp", "factor"), None, None, None),
            P("factor", "fsdp"),
            P("factor", None),
            P("fsdp", "factor"),
        ),
        check_vma=False,
    )
```

```python
import jax
import jax.numpy as jnp
from jax import lax
from jax.experimental import pallas as pl
from jax.experimental.pallas import tpu as pltpu
from jax.sharding import PartitionSpec as P

MESH = pl.DeviceIdType.MESH
F32 = jnp.float32
BF16 = jnp.bfloat16
X_BLOCKS = ((0, 0), (1, 1), (2, 2), (0, 1), (0, 2), (1, 0), (2, 0))
COUNTS = (5, 5, 5, 7, 7)
SLOTS = (
    1, 22, 15, 25, 4, 21, 20, 2, 23, 11, 28, 14, 5, 17, 8, 13,
    19, 12, 3, 9, 10, 18, 16, 27, -1, -1, -1, 6, 26, 24, 0, 7,
)
IDLE = 12


def kernel(
    x_ref, dy_ref, w_ref, a_inv_ref, g_inv_ref,
    conv_ref, a_ref, g_ref, ng_ref,
    x_all, x_t, xa_t, xb, z_all, z_sh, w_all, a_acc, inv_both,
    m_part, m_recv, m_cols, m_piece, m_rows, n_send, n_recv,
    a_send, a_recv, a_sum, tile, g_send, g_recv, g_sum, g2_recv, g_piece, g_fin,
    c_send, c_recv,
    in_sem, inv_sem, xs_sem, xr_sem, xh_sem, xf_sem, zs_sem, zr_sem, zf_sem, ws_sem, wr_sem, wf_sem,
    ms_sem, mr_sem, mxs_sem, mxr_sem, mgs_sem, mgr_sem, ns_sem, nr_sem, as_sem, ar_sem, ts_sem, tr_sem,
    gs_sem, gr_sem, g2s_sem, g2r_sem, g3s_sem, g3r_sem, cs_sem, cr_sem,
):
    i = lax.axis_index("fsdp")
    j = lax.axis_index("factor")
    xh, y, core = j // 8, (j // 2) % 4, j % 2
    a = 2 * xh + core
    b = y
    sibling = j + 1 - 2 * core
    xl, z = i // 8, i % 8

    def remote(src, dst, send, recv, dev_i, dev_j):
        return pltpu.make_async_remote_copy(
            src_ref=src, dst_ref=dst, send_sem=send, recv_sem=recv,
            device_id=(dev_i, dev_j), device_id_type=MESH,
        )

    def each(lo, hi, body):
        def step(k, carry):
            body(k)
            return carry
        lax.fori_loop(lo, hi, step, 0)

    entry = pltpu.get_barrier_semaphore()

    def greet(k):
        pl.semaphore_signal(entry, inc=1, device_id=((i + k) % 16, j), device_id_type=MESH)
        pl.semaphore_signal(entry, inc=1, device_id=(i, (j + k) % 16), device_id_type=MESH)

    each(1, 16, greet)
    pl.semaphore_wait(entry, 30)
    each(1, 16, lambda k: pl.semaphore_signal(
        in_sem, inc=1, device_id=(i, (j + k) % 16), device_id_type=MESH))

    def image(half, step):
        return 8 * ((xh + half) % 2) + 2 * ((y + step + 4) % 4) + core

    def x_at(who, lo=0, size=256):
        return x_all.at[who, pl.ds(16 + lo, size)]

    def x_own(n):
        to = (image(0, 1), image(0, -1), image(1, 0), sibling)[n]
        return remote(x_ref, x_at(j), xs_sem.at[n], xr_sem.at[j], i, to)

    def x_pass(n):
        who = image(1, 0)
        return remote(x_at(who), x_at(who), xs_sem.at[4 + n], xr_sem.at[who], i, image(0, 1 - 2 * n))

    def x_half(half, n):
        step = 1 - 2 * n
        who = image(half, -step)
        here = x_at(who, 128 * n, 128)
        return remote(here, here, xs_sem.at[6 + 2 * half + n], (xr_sem, xh_sem)[n].at[who], i, image(0, step))

    def x_fwd(who):
        return remote(x_at(who), x_at(who), xf_sem.at[who], xr_sem.at[who], i, sibling)

    def x_got(who, lo=0, size=256, sem=None):
        here = x_at(who, lo, size)
        remote(here, here, xf_sem.at[who], (xr_sem if sem is None else sem).at[who], i, sibling).wait_recv()

    for n in range(4):
        x_own(n).start()

    def z_out(k):
        to = (j + 2 * k) % 16
        return remote(dy_ref.at[:, pl.ds(pl.multiple_of(128 * ((to // 2) % 4), 128), 128)],
                      z_all.at[j], zs_sem.at[k], zr_sem.at[j], i, to)

    each(1, 8, lambda k: z_out(k).start())
    here_y = pl.ds(pl.multiple_of(128 * y, 128), 128)
    z_sib = remote(dy_ref.at[:, here_y], z_all.at[j], zs_sem.at[0], zr_sem.at[j], i, sibling)
    z_sib.start()

    def w_at(who):
        return w_all.at[pl.ds(pl.multiple_of(288 * who, 32), 288)]

    def w_out(k):
        return remote(w_ref.at[:, here_y], w_at(i), ws_sem.at[k], wr_sem.at[i], (i + k) % 16, j)

    w_lo = 2 - core

    def w_each(body):
        def step(n, carry):
            body(2 * n + w_lo)
            return carry
        lax.fori_loop(0, 7 + core, step, 0)

    inv_out = remote(a_inv_ref, inv_both.at[xl], inv_sem.at[0], inv_sem.at[1], (i + 8) % 16, j)

    def clear(who):
        x_all[pl.ds(who, 1), 0:16] = jnp.zeros((1, 16, 512), BF16)
        x_all[pl.ds(who, 1), 272:288] = jnp.zeros((1, 16, 512), BF16)

    each(0, 16, clear)
    x_all[pl.ds(j, 1), 16:272] = x_ref[...][None]
    z_all[pl.ds(j, 1)] = dy_ref[:, here_y][None]
    w_all[pl.ds(pl.multiple_of(288 * i, 32), 288), :] = w_ref[:, here_y]
    inv_both[pl.ds(xl, 1)] = a_inv_ref[...][None]
    xb[256:288, :] = jnp.zeros((32, 384), BF16)
    for dx in range(3):
        z_sh[dx, 0:16] = jnp.zeros((16, 128), BF16)
        z_sh[dx, 272:288] = jnp.zeros((16, 128), BF16)
    a_acc[...] = jnp.zeros((5, 384, 384), F32)
    m_part[...] = jnp.zeros((1152, 128), F32)

    col = lax.broadcasted_iota(jnp.int32, (128, 256), 1) % 16
    row = lax.broadcasted_iota(jnp.int32, (256, 128), 0) % 16
    map_row = lax.broadcasted_iota(jnp.int32, (256, 384), 0) // 16
    none = jnp.zeros((256, 384), BF16)

    def terms(who):
        x_t[...] = x_all[pl.ds(who, 1), 16:272].reshape(256, 512).T
        mid = x_t[pl.ds(pl.multiple_of(128 * a, 128), 128), :]
        wide = mid.astype(F32)
        xa_t[0:128] = jnp.where(col == 0, 0.0, pltpu.roll(wide, 1, 1)).astype(BF16)
        xa_t[128:256] = mid
        xa_t[256:384] = jnp.where(col == 15, 0.0, pltpu.roll(wide, 255, 1)).astype(BF16)
        mid = x_all[pl.ds(who, 1), 16:272, here_y].reshape(256, 128)
        wide = mid.astype(F32)
        xb[0:256, 0:128] = jnp.where(row == 0, 0.0, pltpu.roll(wide, 1, 0)).astype(BF16)
        xb[0:256, 128:256] = mid
        xb[0:256, 256:384] = jnp.where(row == 15, 0.0, pltpu.roll(wide, 255, 0)).astype(BF16)
        mid = z_all[pl.ds(who, 1)].reshape(256, 128)
        wide = mid.astype(F32)
        z_sh[0, 16:272] = jnp.where(row == 15, 0.0, pltpu.roll(wide, 255, 0)).astype(BF16)
        z_sh[1, 16:272] = mid
        z_sh[2, 16:272] = jnp.where(row == 0, 0.0, pltpu.roll(wide, 1, 0)).astype(BF16)
        lhs = xa_t[...]
        flat = xb[0:256, :]
        a_acc[0] += jnp.dot(lhs, jnp.where(map_row == 15, none, flat), preferred_element_type=F32)
        a_acc[1] += jnp.dot(lhs, flat, preferred_element_type=F32)
        a_acc[2] += jnp.dot(lhs, jnp.where(map_row == 0, none, flat), preferred_element_type=F32)
        a_acc[3] += jnp.dot(lhs, xb[16:272, :], preferred_element_type=F32)
        a_acc[4] += jnp.dot(lhs, xb[32:288, :], preferred_element_type=F32)
        for k in range(9):
            r = 9 * a + k
            tap = r // 4
            part = jnp.dot(x_t[pl.ds(pl.multiple_of(128 * (r % 4), 128), 128), :],
                           z_sh[tap % 3, pl.ds(pl.multiple_of(32 - 16 * (tap // 3), 16), 256), :],
                           preferred_element_type=F32)
            m_part[128 * k:128 * k + 128, :] += part

    def z_fwd(who):
        return remote(z_all.at[who], z_all.at[who], zf_sem.at[who // 2], zr_sem.at[who], i, sibling)

    def z_got(who):
        remote(z_all.at[who], z_all.at[who], zf_sem.at[0], zr_sem.at[who], i, sibling).wait_recv()

    def hand_on(who):
        x_fwd(who).start()
        z_got(who)
        z_fwd(who).start()

    def from_ring(half, n):
        x_got(image(half, 2 * n - 1))
        x_half(half, n).start()
        hand_on(image(half, 2 * n - 1))

    def from_far(half):
        who = image(half, 2)
        x_got(who, 0, 128)
        x_got(who, 128, 128, xh_sem)
        hand_on(who)

    def arrivals(n, carry):
        @pl.when(n == 1)
        def _():
            from_ring(0, 0)
            from_ring(0, 1)
            x_got(image(1, 0))
            x_pass(0).start()
            x_pass(1).start()
            hand_on(image(1, 0))
            w_each(lambda k: w_out(k).start())

        @pl.when(n == 3)
        def _():
            from_far(0)

        @pl.when(n == 5)
        def _():
            from_ring(1, 0)
            from_ring(1, 1)

        @pl.when(n == 7)
        def _():
            from_far(1)

        half = jnp.where((n == 3) | (n > 4), 1, 0)
        step = jnp.where((n == 0) | (n == 3), 0, jnp.where((n == 1) | (n == 5), 3, jnp.where((n == 2) | (n == 6), 1, 2)))
        mine = image(half, step)

        def one(c, carry):
            who = jnp.where(c == 0, mine, mine + 1 - 2 * core)

            @pl.when(c == 1)
            def _():
                x_got(who)
                z_got(who)

            terms(who)
            return carry

        return lax.fori_loop(0, 2, one, carry)

    lax.fori_loop(0, 8, arrivals, 0)

    def w_in(k):
        src = (i + 16 - k) % 16
        remote(w_at(src), w_at(src), ws_sem.at[k], wr_sem.at[src], src, j).wait_recv()

    def w_fwd(k):
        src = (i + 16 - k) % 16
        return remote(w_at(src), w_at(src), wf_sem.at[k], wr_sem.at[src], i, sibling)

    def w_forward(k):
        w_in(k)
        w_fwd(k).start()

    def far_first(k):
        n = k - 1 + k // 15
        t = n // 2
        dz = jnp.where(t % 2 == 0, 4 + t // 2, 4 - (t + 1) // 2)
        return 8 * ((xl + n % 2) % 2) + (z + dz) % 8

    def m_out(k):
        to = far_first(k)
        return remote(m_part.at[pl.ds(pl.multiple_of(72 * to, 8), 72)], m_recv.at[i],
                      ms_sem.at[k], mr_sem.at[i], to, j)

    each(1, 16, lambda k: m_out(k).start())
    inv_out.start()
    m_recv[pl.ds(i, 1)] = m_part[pl.ds(pl.multiple_of(72 * i, 8), 72)][None]

    cot = dy_ref[...]
    g_send[...] = lax.dot_general(
        cot, cot, (((0,), (0,)), ((), ())), preferred_element_type=F32).astype(BF16)

    def g_out(k):
        to = (j + k) % 16
        return remote(g_send.at[pl.ds(pl.multiple_of(32 * to, 32), 32)], g_recv.at[j],
                      gs_sem.at[k], gr_sem.at[j], i, to)

    each(1, 16, lambda k: g_out(k).start())
    g_recv[pl.ds(j, 1)] = g_send[pl.ds(pl.multiple_of(32 * j, 32), 32)][None]

    own_slot = (i + 11 * j) % 16

    def a_to(slot):
        return (slot + 5 * j) % 16

    def a_out(slot):
        return remote(a_send.at[pl.ds(pl.multiple_of(256 * slot, 256), 256)], a_recv.at[i],
                      as_sem.at[slot], ar_sem.at[i], a_to(slot), j)

    def a_start(k):
        slot = (far_first(k) + 11 * j) % 16

        @pl.when(slot != IDLE)
        def _():
            a_out(slot).start()

    at_block = 0
    for combo, count in enumerate(COUNTS):
        part = a_acc[combo]
        for row_x, col_x in X_BLOCKS[:count]:
            spot = 128 * SLOTS.index(at_block)
            a_send[spot:spot + 128, :] = part[
                128 * row_x:128 * row_x + 128, 128 * col_x:128 * col_x + 128].astype(BF16)
            at_block += 1
    for spot, block in enumerate(SLOTS):
        if block < 0:
            a_send[128 * spot:128 * spot + 128, :] = jnp.zeros((128, 128), BF16)

    @pl.when(own_slot != IDLE)
    def _():
        a_recv[pl.ds(i, 1)] = a_send[pl.ds(pl.multiple_of(256 * own_slot, 256), 256)][None]

    w_each(w_forward)

    def w_other(k):
        @pl.when(k % 2 != core)
        def _():
            w_in(k)

    each(1, 16, w_other)
    conv_row = lax.broadcasted_iota(jnp.int32, (256, 128), 0) % 16

    def conv_image(q):
        who = 8 * xh + 2 * q + core
        parts = []
        for dx in range(3):
            total = jnp.zeros((256, 128), F32)
            for dy in range(3):
                total = total + jnp.dot(
                    x_all[pl.ds(who, 1), 16 * dy:16 * dy + 256].reshape(256, 512),
                    w_all[512 * (3 * dy + dx):512 * (3 * dy + dx) + 512, :],
                    preferred_element_type=F32)
            parts.append(total)
        out = parts[1] + jnp.where(conv_row == 0, 0.0, pltpu.roll(parts[0], 1, 0))
        out = out + jnp.where(conv_row == 15, 0.0, pltpu.roll(parts[2], 255, 0))
        c_send[pl.ds(q, 1)] = out.astype(BF16)[None]

    each(0, 4, conv_image)

    def c_out(k):
        q = (y + k) % 4
        return remote(c_send.at[q], c_recv.at[:, here_y], cs_sem.at[k], cr_sem.at[y],
                      i, 8 * xh + 2 * q + core)

    each(1, 4, lambda k: c_out(k).start())
    c_recv[:, here_y] = c_send[y]

    each(1, 16, a_start)

    def m_in(k):
        src = (i + 16 - k) % 16
        here = m_recv.at[src]
        remote(here, here, ms_sem.at[k], mr_sem.at[src], src, j).wait_recv()

    each(1, 16, m_in)
    total = m_recv[0]
    for k in range(1, 16):
        total = total + m_recv[k]
    m_cols[pl.ds(y, 1)] = total[None]

    def mx_out(k):
        return remote(m_cols.at[y], m_cols.at[y], mxs_sem.at[k], mxr_sem.at[y], i, image_of(k))

    def image_of(k):
        return 8 * xh + 2 * ((y + k) % 4) + core

    each(1, 4, lambda k: mx_out(k).start())
    pl.semaphore_wait(in_sem, 15)

    def mx_in(k):
        src = (y + 4 - k) % 4
        remote(m_cols.at[src], m_cols.at[src], mxs_sem.at[k], mxr_sem.at[src], i, sibling).wait_recv()

    each(1, 4, mx_in)
    total = jnp.zeros((72, 128), F32)
    for q in range(4):
        total = total + jnp.dot(m_cols[q], g_inv_ref[128 * q:128 * q + 128, here_y],
                                precision=lax.Precision.HIGHEST, preferred_element_type=F32)
    m_piece[...] = total
    m_to = 4 * a + i // 4

    def m_spot(rho, chunk):
        return m_rows.at[pl.ds(pl.multiple_of(72 * rho, 8), 72),
                         pl.ds(pl.multiple_of(128 * chunk, 128), 128)]

    m_here = 2 * (i % 4) + b % 2

    def mg_out(n):
        return remote(m_piece, m_spot(i % 4, b % 2), mgs_sem.at[n], mgr_sem.at[m_here], 8 * (b // 2) + n, m_to)

    def mg_mine(n):
        return (8 * (b // 2) + n == i) & (m_to == j)

    def mg_start(k):
        n = (z + k) % 8

        @pl.when(jnp.logical_not(mg_mine(n)))
        def _():
            mg_out(n).start()

        @pl.when(mg_mine(n))
        def _():
            pltpu.make_async_copy(m_piece, m_spot(i % 4, b % 2), mgr_sem.at[m_here]).start()

    each(0, 8, mg_start)

    def g_in(k):
        src = (j + 16 - k) % 16
        here = g_recv.at[src]
        remote(here, here, gs_sem.at[k], gr_sem.at[src], i, src).wait_recv()

    each(1, 16, g_in)
    total = g_recv[0].astype(F32)
    for k in range(1, 16):
        total = total + g_recv[k].astype(F32)
    g_sum[...] = total

    def g_spot(ref, who):
        return ref.at[pl.ds(pl.multiple_of(8 * (who // 4), 8), 8),
                      pl.ds(pl.multiple_of(128 * (who % 4), 128), 128)]

    def g2_out(k):
        to = (i + k) % 16
        return remote(g_spot(g_sum, to), g2_recv.at[i], g2s_sem.at[k], g2r_sem.at[i], to, j)

    each(1, 16, lambda k: g2_out(k).start())
    g2_recv[pl.ds(i, 1)] = g_sum[pl.ds(pl.multiple_of(8 * (i // 4), 8), 8),
                                 pl.ds(pl.multiple_of(128 * (i % 4), 128), 128)][None]

    @pl.when(own_slot != IDLE)
    def _():
        def a_in(k):
            src = (i + 16 - k) % 16
            here = a_recv.at[src]
            remote(here, here, as_sem.at[0], ar_sem.at[src], src, j).wait_recv()

        each(1, 16, a_in)
        for half in range(2):
            span = slice(128 * half, 128 * half + 128)
            total = a_recv[0, span].astype(F32)
            for k in range(1, 16):
                total = total + a_recv[k, span].astype(F32)
            a_sum[2 * half] = total
            a_sum[2 * half + 1] = total.T

    def block_in(slot):
        block = jnp.int32(-1)
        for spot, held in enumerate(SLOTS):
            block = jnp.where(slot == spot, held, block)
        return block

    def spread(act):
        for half in range(2):
            k = block_in(2 * own_slot + half)
            flat = k < 15
            ey = jnp.where(flat, 0, jnp.where(k < 22, 1, 2))
            s = jnp.where(flat, (k + 5) % 5, (k + 6) % 7)
            ex = jnp.where(s < 3, 0, jnp.where(s < 5, s - 2, 4 - s))
            low_x = jnp.where(s < 3, s, jnp.where(s < 5, 0, s - 4))
            low_y = jnp.where(flat, (k + 5) // 5 - 1, 0)

            def place(n):
                turned, yp, xp = n // 4, (n // 2) % 2, n % 2
                ok = (k >= 0) & ((yp == 0) | (ey == 1)) & ((xp == 0) | (ex == 1) | (ex == -1))
                ok = ok & ((turned == 0) | (ey != 0) | (ex != 0))

                @pl.when(ok)
                def _():
                    row_y, row_x = low_y + yp, low_x + xp
                    first = 4 * (3 * row_y + row_x) + a
                    second = 4 * (3 * (row_y + ey) + row_x + ex) + b
                    r = jnp.where(turned == 0, first, second)
                    c = jnp.where(turned == 0, second, first)
                    src = a_sum.at[2 * half + turned]
                    for t in range(4):
                        to_j = (4 * r) // 9 + t // 2
                        to_i = (4 * c) // 9 + t % 2
                        inside = (to_j <= (128 * r + 127) // 288) & (to_i <= (128 * c + 127) // 288)
                        at_r = r - (9 * to_j) // 4
                        at_c = c - (9 * to_i) // 4
                        mine = (to_i == i) & (to_j == j)

                        @pl.when(inside)
                        def _():
                            dst = tile.at[pl.ds(pl.multiple_of(128 * at_r, 128), 128),
                                          pl.ds(pl.multiple_of(128 * at_c, 128), 128)]
                            arrived = tr_sem.at[3 * at_r + at_c]

                            @pl.when(jnp.logical_not(mine))
                            def _():
                                act(remote(src, dst, ts_sem.at[32 * half + 4 * n + t], arrived, to_i, to_j))

                            if act is start:
                                @pl.when(mine)
                                def _():
                                    pltpu.make_async_copy(src, dst, arrived).start()

            each(0, 8, place)

    def start(copy):
        copy.start()

    def sent_off(copy):
        copy.wait_send()

    spread(start)

    for q in range(8):
        here = m_spot(q // 2, q % 2)
        remote(here, here, mgs_sem.at[0], mgr_sem.at[q], i, sibling).wait_recv()
    inv_out.wait_recv()
    lane = lax.broadcasted_iota(jnp.int32, (72, 128), 1) // 32
    for t in range(2):
        prod = jnp.dot(inv_both[t], m_rows[...], precision=lax.Precision.HIGHEST,
                       preferred_element_type=F32)
        for to in range(8):
            piece = jnp.zeros((72, 128), F32)
            for q in range(4):
                block = prod[72 * q:72 * q + 72, 128 * (to // 4):128 * (to // 4) + 128]
                shift = (32 * (q - to % 4)) % 128
                if shift:
                    block = pltpu.roll(block, shift, 1)
                piece = jnp.where(lane == q, block, piece)
            n_send[8 * t + to] = piece
    def n_out(n):
        return remote(n_send.at[n], n_recv.at[j], ns_sem.at[n], nr_sem.at[j], 8 * (n // 8) + z, 8 * xl + n % 8)

    def n_mine(n):
        return (n // 8 == xl) & (8 * xl + n % 8 == j)

    def n_start(k):
        n = (k + j) % 16

        @pl.when(jnp.logical_not(n_mine(n)))
        def _():
            n_out(n).start()

    each(0, 16, n_start)

    @pl.when(xl == j // 8)
    def _():
        n_recv[pl.ds(j, 1)] = n_send[pl.ds(j, 1)]

    def g2_in(k):
        src = (i + 16 - k) % 16
        here = g2_recv.at[src]
        remote(here, here, g2s_sem.at[k], g2r_sem.at[src], src, j).wait_recv()

    each(1, 16, g2_in)
    total = g2_recv[0]
    for k in range(1, 16):
        total = total + g2_recv[k]
    g_piece[...] = total

    def g3_out(k):
        return remote(g_piece, g_spot(g_fin, i), g3s_sem.at[k], g3r_sem.at[i], (i + k) % 16, j)

    each(1, 16, lambda k: g3_out(k).start())
    g_fin[pl.ds(pl.multiple_of(8 * (i // 4), 8), 8),
          pl.ds(pl.multiple_of(128 * (i % 4), 128), 128)] = total

    def c_in(k):
        q = (y + 4 - k) % 4
        here = c_recv.at[:, pl.ds(pl.multiple_of(128 * q, 128), 128)]
        remote(here, here, cs_sem.at[k], cr_sem.at[q], i, sibling).wait_recv()

    each(1, 4, c_in)
    conv_ref[...] = c_recv[...]

    for q in range(9):
        here = tile.at[pl.ds(128 * (q // 3), 128), pl.ds(128 * (q % 3), 128)]
        remote(here, here, ts_sem.at[0], tr_sem.at[q], i, sibling).wait_recv()
    rows = tile[pl.ds(pl.multiple_of(32 * (j % 4), 32), 288), :]
    rows = pltpu.roll(rows, (384 - 32 * (i % 4)) % 384, 1)[:, 0:288]
    a_ref[...] = rows

    def g3_in(k):
        src = (i + 16 - k) % 16
        here = g_spot(g_fin, src)
        remote(here, here, g3s_sem.at[k], g3r_sem.at[src], src, j).wait_recv()

    each(1, 16, g3_in)
    g_ref[...] = g_fin[...]

    def n_in(src):
        @pl.when(jnp.logical_not((src == j) & (xl == j // 8)))
        def _():
            here = n_recv.at[src]
            remote(here, here, ns_sem.at[0], nr_sem.at[src], i, sibling).wait_recv()

    each(0, 16, n_in)
    total = n_recv[0]
    for k in range(1, 16):
        total = total + n_recv[k]
    ng_ref[...] = total

    for n in range(4):
        x_own(n).wait_send()
    for n in range(2):
        x_pass(n).wait_send()
        x_half(0, n).wait_send()
        x_half(1, n).wait_send()
    inv_out.wait_send()
    z_sib.wait_send()
    each(1, 8, lambda k: z_out(k).wait_send())

    def handed(k):
        who = (j + 2 * k) % 16
        x_fwd(who).wait_send()
        z_fwd(who).wait_send()

    each(1, 8, handed)
    w_each(lambda k: w_out(k).wait_send())
    w_each(lambda k: w_fwd(k).wait_send())
    each(1, 4, lambda k: mx_out(k).wait_send())
    each(1, 4, lambda k: c_out(k).wait_send())

    def rest_sent(k):
        g_out(k).wait_send()
        m_out(k).wait_send()
        g2_out(k).wait_send()
        g3_out(k).wait_send()

    each(1, 16, rest_sent)

    def a_sent(slot):
        @pl.when((slot != IDLE) & (slot != own_slot))
        def _():
            a_out(slot).wait_send()

    each(0, 16, a_sent)

    def mg_sent(n):
        @pl.when(jnp.logical_not(mg_mine(n)))
        def _():
            mg_out(n).wait_send()

    each(0, 8, mg_sent)

    def n_sent(n):
        @pl.when(jnp.logical_not(n_mine(n)))
        def _():
            n_out(n).wait_send()

    each(0, 16, n_sent)
    spread(sent_off)


def finish(conv_ref, a_sum_ref, g_sum_ref, packed_ref, a_old_ref, g_old_ref, out_ref, a_ref, g_ref, ng_ref):
    out_ref[...] = conv_ref[...]
    a_ref[...] = 0.5 * a_old_ref[...] + (0.5 / 65536.0) * a_sum_ref[...]
    g_ref[...] = 0.5 * g_old_ref[...] + 0.5 * g_sum_ref[...]
    packed = packed_ref[...]
    rows = [packed[:, 0:32]] + [pltpu.roll(packed, 128 - 32 * q, 1)[:, 0:32] for q in range(1, 4)]
    ng_ref[...] = jnp.concatenate(rows, axis=0).T.astype(BF16)


def per_device(activations, cotangent, weight, a_factor_old, g_factor_old, a_inverse, g_inverse):
    vmem = pl.BlockSpec(memory_space=pltpu.VMEM)
    dma = pltpu.SemaphoreType.DMA
    conv, a_factor, g_factor, packed = pl.pallas_call(
        kernel,
        name="kfac_step",
        out_shape=(
            jax.ShapeDtypeStruct((256, 512), BF16),
            jax.ShapeDtypeStruct((288, 288), F32),
            jax.ShapeDtypeStruct((32, 512), F32),
            jax.ShapeDtypeStruct((72, 128), F32),
        ),
        in_specs=[vmem] * 5,
        out_specs=(vmem,) * 4,
        scratch_shapes=[
            pltpu.VMEM((16, 288, 512), BF16),
            pltpu.VMEM((512, 256), BF16),
            pltpu.VMEM((384, 256), BF16),
            pltpu.VMEM((288, 384), BF16),
            pltpu.VMEM((16, 256, 128), BF16),
            pltpu.VMEM((3, 288, 128), BF16),
            pltpu.VMEM((4608, 128), BF16),
            pltpu.VMEM((5, 384, 384), F32),
            pltpu.VMEM((2, 288, 288), F32),
            pltpu.VMEM((1152, 128), F32),
            pltpu.VMEM((16, 72, 128), F32),
            pltpu.VMEM((4, 72, 128), F32),
            pltpu.VMEM((72, 128), F32),
            pltpu.VMEM((288, 256), F32),
            pltpu.VMEM((16, 72, 128), F32),
            pltpu.VMEM((16, 72, 128), F32),
            pltpu.VMEM((4096, 128), BF16),
            pltpu.VMEM((16, 256, 128), BF16),
            pltpu.VMEM((4, 128, 128), F32),
            pltpu.VMEM((384, 384), F32),
            pltpu.VMEM((512, 512), BF16),
            pltpu.VMEM((16, 32, 512), BF16),
            pltpu.VMEM((32, 512), F32),
            pltpu.VMEM((16, 8, 128), F32),
            pltpu.VMEM((8, 128), F32),
            pltpu.VMEM((32, 512), F32),
            pltpu.VMEM((4, 256, 128), BF16),
            pltpu.VMEM((256, 512), BF16),
            pltpu.SemaphoreType.REGULAR,
            dma((2,)),
            dma((10,)), dma((16,)), dma((16,)), dma((16,)),
            dma((8,)), dma((16,)), dma((8,)),
            dma((16,)), dma((16,)), dma((16,)),
            dma((16,)), dma((16,)), dma((4,)), dma((4,)), dma((16,)), dma((16,)),
            dma((16,)), dma((16,)),
            dma((16,)), dma((16,)), dma((64,)), dma((9,)),
            dma((16,)), dma((16,)), dma((16,)), dma((16,)), dma((16,)), dma((16,)),
            dma((4,)), dma((4,)),
        ],
        compiler_params=pltpu.CompilerParams(
            collective_id=0, has_side_effects=True, vmem_limit_bytes=56 * 1024 * 1024),
        cost_estimate=pl.CostEstimate(flops=15_000_000_000, bytes_accessed=4_000_000, transcendentals=0),
    )(activations.reshape(256, 512), cotangent.reshape(256, 512), weight, a_inverse, g_inverse)
    conv, a_factor, g_factor, natural = pl.pallas_call(
        finish,
        name="finish",
        out_shape=(
            jax.ShapeDtypeStruct((256, 512), BF16),
            jax.ShapeDtypeStruct((288, 288), F32),
            jax.ShapeDtypeStruct((32, 512), F32),
            jax.ShapeDtypeStruct((32, 288), BF16),
        ),
        in_specs=[vmem] * 6,
        out_specs=(vmem,) * 4,
        cost_estimate=pl.CostEstimate(flops=1_000_000, bytes_accessed=2_000_000, transcendentals=0),
    )(conv, a_factor, g_factor, packed, a_factor_old, g_factor_old)
    return conv.reshape(1, 16, 16, 512), a_factor, g_factor, natural.T


def solution(mesh):
    return jax.shard_map(
        per_device,
        mesh=mesh,
        in_specs=(
            P(("fsdp", "factor"), None, None, None),
            P(("fsdp", "factor"), None, None, None),
            P("fsdp", None),
            P("factor", "fsdp"),
            P("factor", None),
            P("fsdp", "factor"),
            P(),
        ),
        out_specs=(
            P(("fsdp", "factor"), None, None, None),
            P("factor", "fsdp"),
            P("factor", None),
            P("fsdp", "factor"),
        ),
        check_vma=False,
    )
```
